128 devices in a mesh: dp: 4 (over z), ctx: 32 (over x, y, core).
Axes of the slice: x: 4, y: 4, z: 4, core: 2. Of those that a mesh axis runs over, the one named last changes fastest.
Arguments:
- mamba_in: bfloat16 [4, 4096, 3584], P('dp', 'ctx'), may hold values from -30 to 30
- step_raw: float32 [4, 56, 4096], P('dp', None, 'ctx'), may hold values from -3 to 15
- state_in: bfloat16 [4, 4096, 64], P('dp', 'ctx'), may hold values from -0.75 to 0.75
- state_out: bfloat16 [4, 4096, 64], P('dp', 'ctx'), may hold values from -6 to 6
- log_rate: float32 [56], replicated, may hold values from -7.5 to 1.6
- step_bias: float32 [56], replicated, may hold values from -6 to -4.5
- skip_gain: float32 [56], replicated, may hold values from 0.5 to 1.5
- norm_gain: float32 [3584], replicated, may hold values from 0.5 to 1.5
- doc_lengths: int32 [4, 32, 8], P('dp'), may hold values from 1 to 64, as said below
- doc_moved: int32 [4, 32, 8], P('dp'), may hold values from 0 to 1, as said below
- queries: bfloat16 [4, 4096, 3584], P('dp', 'ctx'), may hold values from -16 to 16
- attn_keys: bfloat16 [4, 4096, 3584], P('dp', 'ctx'), may hold values from -16 to 16
- attn_grad: bfloat16 [4, 6144, 3584], P('dp', 'ctx'), may hold values from -12 to 12
Outputs:
- attn_out: bfloat16 [4, 6144, 3584], P('dp', 'ctx')
- grad_queries: bfloat16 [4, 4096, 3584], P('dp', 'ctx')
- grad_keys: bfloat16 [4, 4096, 3584], P('dp', 'ctx')
- grad_mamba_in: bfloat16 [4, 4096, 3584], P('dp', 'ctx')
- grad_state_in: bfloat16 [4, 4096, 64], P('dp', 'ctx')
- grad_state_out: bfloat16 [4, 4096, 64], P('dp', 'ctx')
- grad_step: float32 [4, 56, 4096], P('dp', None, 'ctx')
- grad_heads: float32 [3, 56], replicated
- grad_gain: float32 [3584], replicated
The draws below stay inside these ranges and needn't reach their ends.
Inputs may be any that keep to these rules, and one draw needn't show every extreme that they name: `doc_lengths`: in every row the 8 lengths sum to 128, and the longest is exactly 64. `doc_moved`: the documents marked 1 in one row hold at most 64 positions together, exactly 64 in some row of every draw.
All inputs are finite; a program needn't handle non-finite values.
Results may differ from the reference program's by a relative error of at most 0.0078.
Values may be sent and summed in bfloat16 or wider, within the bound.
No kernel may reach another device: no remote copies, remote signals or barrier semaphores. Data moves between devices by JAX's collectives and lax.ppermute only.
A program may use at most 192 MiB of HBM per device.

```python
import math
import jax
import jax.numpy as jnp
from jax import lax

MAMBA_HEADS = 56
HEAD_SIZE = 64
STATE_SIZE = 64
ATTN_HEADS = 16
TOK_DEV = 128
DOCS_DEV = 8
MAMBA_WIDTH = 3584
ATTN_WIDTH = 3584
SEQUENCE_LENGTH = 4096
DOC_MAX = 64
SEND_MAX = 64
ROWS_ATT = 192
N_DP = 4
N_CTX = 32


def doc_table(key):
    key = jax.random.fold_in(key, 101)
    rows = N_DP * N_CTX
    rest = TOK_DEV - DOC_MAX
    cut_key, order_key, mode_key, coin_key, force_key = jax.random.split(key, 5)
    scores = jax.random.randint(cut_key, (rows, rest - 1), 0, 1 << 20) * rest + jnp.arange(rest - 1, dtype=jnp.int32)[None, :]
    chosen = jnp.argsort(scores, axis=1)[:, :DOCS_DEV - 2].astype(jnp.int32) + 1
    cuts = jnp.sort(chosen, axis=1)
    bounds = jnp.concatenate([jnp.zeros((rows, 1), jnp.int32), cuts, jnp.full((rows, 1), rest, jnp.int32)], axis=1)
    pieces = bounds[:, 1:] - bounds[:, :-1]
    lengths = jnp.concatenate([pieces, jnp.full((rows, 1), DOC_MAX, jnp.int32)], axis=1)
    order_scores = jax.random.randint(order_key, (rows, DOCS_DEV), 0, 1 << 20) * DOCS_DEV + jnp.arange(DOCS_DEV, dtype=jnp.int32)[None, :]
    order = jnp.argsort(order_scores, axis=1)
    lengths = jnp.take_along_axis(lengths, order, axis=1)
    longest = order == DOCS_DEV - 1
    modes = jax.random.randint(mode_key, (rows, 1), 0, 3)
    forced = jax.random.randint(force_key, (), 0, rows)
    modes = jnp.where(jnp.arange(rows, dtype=jnp.int32)[:, None] == forced, 0, modes)
    coins = jax.random.randint(coin_key, (rows, DOCS_DEV), 0, 2)
    moved = jnp.where(longest, modes == 0, (modes == 1) & (coins == 1)).astype(jnp.int32)
    return (lengths.reshape(N_DP, N_CTX, DOCS_DEV), moved.reshape(N_DP, N_CTX, DOCS_DEV))


def draw_doc_lengths(key, part):
    return doc_table(key)[0]


def draw_doc_moved(key, part):
    return doc_table(key)[1]


def draw_mamba_in(key, part):
    key = jax.random.fold_in(key, 3)
    value_key, column_key, row_key = jax.random.split(key, 3)
    shape = (N_DP, SEQUENCE_LENGTH, MAMBA_WIDTH)
    column_scale = jnp.exp(jax.random.uniform(column_key, (1, 1, MAMBA_WIDTH), jnp.float32, -1.15, 1.15))
    row_scale = jnp.exp(jax.random.uniform(row_key, (N_DP, SEQUENCE_LENGTH, 1), jnp.float32, -1.15, 1.15))
    drawn_numbers = jnp.clip(jax.random.normal(value_key, shape, jnp.float32), -3.0, 3.0)
    return jnp.clip(drawn_numbers * column_scale * row_scale, -30.0, 30.0).astype(jnp.bfloat16)


def draw_step_raw(key, part):
    key = jax.random.fold_in(key, 7)
    jitter_random_key, offset_random_key, spike_random_key = jax.random.split(key, 3)
    shape = (N_DP, MAMBA_HEADS, SEQUENCE_LENGTH)
    stochastic_perturbation = 0.5 * jax.random.normal(jitter_random_key, shape, jnp.float32)
    displacement_increments = jax.random.uniform(offset_random_key, (N_DP, MAMBA_HEADS, N_CTX, 1), jnp.float32, -0.7, 0.7)
    displacement_increments = jnp.broadcast_to(displacement_increments, (N_DP, MAMBA_HEADS, N_CTX, TOK_DEV)).reshape(shape)
    surge_locations = jax.random.randint(spike_random_key, (N_DP, MAMBA_HEADS, 4), 0, SEQUENCE_LENGTH)
    entry_indices = jnp.arange(SEQUENCE_LENGTH, dtype=jnp.int32)
    sudden_surge_heights = jnp.any(entry_indices[None, None, :, None] == surge_locations[:, :, None, :], axis=3)
    drawn_numbers = jnp.clip(stochastic_perturbation, -2.0, 2.0) + displacement_increments + jnp.where(sudden_surge_heights, 12.0, 0.0)
    return jnp.clip(drawn_numbers, -3.0, 15.0)


def base_rows(key):
    shape = (N_DP, SEQUENCE_LENGTH, ATTN_WIDTH)
    return jnp.clip(jax.random.normal(key, shape, jnp.float32), -4.0, 4.0)


def draw_queries(key, part):
    drawn = base_rows(jax.random.fold_in(key, 13))
    return jnp.clip(drawn, -16.0, 16.0).astype(jnp.bfloat16)


def draw_attn_keys(key, part):
    drawn = base_rows(jax.random.fold_in(key, 17))
    return jnp.clip(drawn, -16.0, 16.0).astype(jnp.bfloat16)


def draw_attn_grad(key, part):
    key = jax.random.fold_in(key, 5)
    value_key = jax.random.fold_in(key, 0)
    shape = (N_DP, N_CTX * ROWS_ATT, ATTN_WIDTH)
    blocks = (jnp.arange(N_CTX * ROWS_ATT, dtype=jnp.int32) // ROWS_ATT).astype(jnp.float32)
    rise = (1.0 + 2.0 * blocks / max(N_CTX - 1, 1))[None, :, None]
    drawn_numbers = jnp.clip(jax.random.normal(value_key, shape, jnp.float32), -4.0, 4.0)
    return jnp.clip(drawn_numbers * rise, -12.0, 12.0).astype(jnp.bfloat16)


def shard_levels(stream_key, extent, cuts, low, high):
    level = 1.0
    for axis_at, shards_of in cuts:
        draws = jax.random.uniform(jax.random.fold_in(jax.random.fold_in(stream_key, 6), axis_at), (shards_of,), jnp.float32, low / len(cuts), high / len(cuts))
        level = level * jnp.repeat(jnp.exp(draws), extent[axis_at] // shards_of).reshape((-1,) + (1,) * (len(extent) - 1 - axis_at))
    return level


def bell_draw(stream_key, dims, scale, most, shards=(), kind=jnp.bfloat16):
    values = scale * jax.random.normal(stream_key, dims, jnp.float32)
    if shards:
        values = values * shard_levels(stream_key, dims, shards, -0.22, 0.18)
    return jnp.clip(values, -most, most).astype(kind)


def setup_inputs(seed: int = 0) -> dict:
    seeds = jax.random.split(jax.random.key(seed), 14)
    return {
        "mamba_in": draw_mamba_in(jax.random.fold_in(seeds[13], 71), 0),
        "step_raw": draw_step_raw(jax.random.fold_in(seeds[13], 71), 0),
        "state_in": bell_draw(seeds[2], (N_DP, SEQUENCE_LENGTH, STATE_SIZE), (STATE_SIZE ** -0.5), 0.75, ((0, 4), (1, 32))),
        "state_out": bell_draw(seeds[3], (N_DP, SEQUENCE_LENGTH, STATE_SIZE), 1.0, 6.0, ((0, 4), (1, 32))),
        "log_rate": jnp.clip(jax.random.uniform(seeds[4], (MAMBA_HEADS,), jnp.float32, -7.5, 1.6), -7.5, 1.6),
        "step_bias": jnp.clip(jax.random.uniform(seeds[5], (MAMBA_HEADS,), jnp.float32, -6.0, -4.5), -6.0, -4.5),
        "skip_gain": jnp.clip(jax.random.uniform(seeds[6], (MAMBA_HEADS,), jnp.float32, 0.5, 1.5), 0.5, 1.5),
        "norm_gain": jnp.clip(1.0 + 0.1 * jax.random.normal(seeds[7], (MAMBA_WIDTH,), jnp.float32), 0.5, 1.5),
        "doc_lengths": draw_doc_lengths(jax.random.fold_in(seeds[13], 71), 0),
        "doc_moved": draw_doc_moved(jax.random.fold_in(seeds[13], 71), 0),
        "queries": draw_queries(jax.random.fold_in(seeds[13], 71), 0),
        "attn_keys": draw_attn_keys(jax.random.fold_in(seeds[13], 71), 0),
        "attn_grad": draw_attn_grad(jax.random.fold_in(seeds[13], 71), 0),
    }


HIGH = lax.Precision.HIGHEST
EPSILON = 1e-05
MASKED = -1e+30

def decay_sums(raw_steps, step_bias, log_rate):
    step_size = jax.nn.softplus(raw_steps + step_bias[:, None])
    rates = -jnp.exp(log_rate)[:, None] * step_size
    return (step_size, jnp.cumsum(rates, axis=1))

def local_states(x_rows, raw_steps, step_bias, log_rate, in_rows):
    tokens, width = x_rows.shape
    heads = raw_steps.shape[0]
    step_size, running = decay_sums(raw_steps, step_bias, log_rate)
    total = jnp.exp(running[:, -1])
    tail = jnp.exp(running[:, -1:] - running) * step_size
    scaled = x_rows.reshape(tokens, heads, width // heads) * jnp.transpose(tail)[:, :, None]
    carry = jnp.einsum('thp,tn->hpn', scaled, in_rows, precision=HIGH)
    return (total, carry)

def local_outputs(x_rows, raw_steps, step_bias, log_rate, skip_gain, in_rows, out_rows, start_state):
    tokens, width = x_rows.shape
    heads = raw_steps.shape[0]
    step_size, running = decay_sums(raw_steps, step_bias, log_rate)
    row_index = jnp.arange(tokens, dtype=jnp.int32)
    causal = row_index[:, None] >= row_index[None, :]
    gaps = jnp.where(causal[None], running[:, :, None] - running[:, None, :], MASKED)
    gram = jnp.dot(out_rows, jnp.transpose(in_rows), precision=HIGH)
    mixing = jnp.exp(gaps) * gram[None] * step_size[:, None, :]
    x_heads = x_rows.reshape(tokens, heads, width // heads)
    inner = jnp.einsum('hts,shp->thp', mixing, x_heads, precision=HIGH)
    carried = jnp.einsum('tn,hpn->thp', out_rows, start_state, precision=HIGH)
    carried = carried * jnp.transpose(jnp.exp(running))[:, :, None]
    result = inner + carried + skip_gain[None, :, None] * x_heads
    return result.reshape(tokens, width)

def normalize(mixed, gain):
    power = lax.optimization_barrier(jnp.mean(mixed * mixed, axis=-1, keepdims=True))
    return mixed * lax.rsqrt(power + EPSILON) * gain

def doc_layout(lengths, moved, tokens):
    ends = jnp.cumsum(lengths).astype(jnp.int32)
    entry_indices = jnp.arange(tokens, dtype=jnp.int32)
    segments = lax.optimization_barrier(jnp.sum((entry_indices[:, None] >= ends[None, :]).astype(jnp.int32), axis=1)).astype(jnp.int32)
    labels = jnp.arange(lengths.shape[0], dtype=jnp.int32)
    moving = lax.optimization_barrier(jnp.sum(jnp.where(segments[:, None] == labels[None, :], moved[None, :], 0), axis=1)).astype(jnp.int32)
    slot_index = (jnp.cumsum(moving) - 1).astype(jnp.int32)
    return (segments, moving, slot_index)

def pick_mask(moving, slot_index, slots):
    targets = jnp.arange(slots, dtype=jnp.int32)
    return (slot_index[None, :] == targets[:, None]) & (moving[None, :] == 1)

def attend(q_rows, k_rows, v_rows, segments, heads):
    rows, width = q_rows.shape
    size = width // heads
    scale = 1.0 / math.sqrt(size)
    q_heads = q_rows.reshape(rows, heads, size).astype(jnp.float32)
    k_heads = k_rows.reshape(rows, heads, size).astype(jnp.float32)
    v_heads = v_rows.reshape(rows, heads, size).astype(jnp.float32)
    scores = jnp.einsum('qhd,khd->hqk', q_heads, k_heads, precision=HIGH) * scale
    row_index = jnp.arange(rows, dtype=jnp.int32)
    allowed = (segments[:, None] == segments[None, :]) & (row_index[None, :] <= row_index[:, None])
    scores = jnp.where(allowed[None], scores, MASKED)
    peak = lax.optimization_barrier(jnp.max(scores, axis=-1, keepdims=True))
    weights = jnp.exp(scores - peak)
    probs = weights / lax.optimization_barrier(jnp.sum(weights, axis=-1, keepdims=True))
    probs_low = probs.astype(jnp.bfloat16)
    mixed = jnp.einsum('hqk,khd->qhd', probs_low.astype(jnp.float32), v_heads, precision=HIGH)
    return (mixed.astype(jnp.bfloat16).reshape(rows, width), probs, probs_low)

def attend_back(q_rows, k_rows, v_rows, probs, probs_low, grad_rows, heads):
    rows, width = q_rows.shape
    size = width // heads
    scale = 1.0 / math.sqrt(size)
    q_heads = q_rows.reshape(rows, heads, size).astype(jnp.float32)
    k_heads = k_rows.reshape(rows, heads, size).astype(jnp.float32)
    v_heads = v_rows.reshape(rows, heads, size).astype(jnp.float32)
    grad_heads = grad_rows.reshape(rows, heads, size).astype(jnp.float32)
    dprobs = jnp.einsum('qhd,khd->hqk', grad_heads, v_heads, precision=HIGH)
    delta = lax.optimization_barrier(jnp.sum(probs * dprobs, axis=-1, keepdims=True))
    dscores = (probs * (dprobs - delta) * scale).astype(jnp.bfloat16).astype(jnp.float32)
    grad_query = jnp.einsum('hqk,khd->qhd', dscores, k_heads, precision=HIGH)
    grad_key = jnp.einsum('hqk,qhd->khd', dscores, q_heads, precision=HIGH)
    grad_value = jnp.einsum('hqk,qhd->khd', probs_low.astype(jnp.float32), grad_heads, precision=HIGH)
    return (grad_query.astype(jnp.bfloat16).reshape(rows, width), grad_key.astype(jnp.bfloat16).reshape(rows, width), grad_value.astype(jnp.bfloat16).reshape(rows, width))

def reference(mamba_in, step_raw, state_in, state_out, log_rate, step_bias, skip_gain, norm_gain, doc_lengths, doc_moved, queries, attn_keys, attn_grad):
    partner = jnp.bitwise_xor(jnp.arange(N_CTX, dtype=jnp.int32), N_CTX // 2)
    out_rows_all, gq_all, gk_all, gx_all, gin_all, gout_all, gstep_all = ([], [], [], [], [], [], [])
    heads_total = jnp.zeros((3, MAMBA_HEADS), jnp.float32)
    gain_total = jnp.zeros((MAMBA_WIDTH,), jnp.float32)
    for sequence in range(N_DP):

        def whole(x_rows, raw_steps, bias, rates, skip, in_rows, out_rows):
            x_blocks = x_rows.reshape(N_CTX, TOK_DEV, MAMBA_WIDTH)
            raw_blocks = jnp.transpose(raw_steps.reshape(MAMBA_HEADS, N_CTX, TOK_DEV), (1, 0, 2))
            in_blocks = in_rows.reshape(N_CTX, TOK_DEV, STATE_SIZE)
            out_blocks = out_rows.reshape(N_CTX, TOK_DEV, STATE_SIZE)

            def advance(state, pieces):
                x_block, raw_block, in_block, out_block = pieces
                mixed = local_outputs(x_block, raw_block, bias, rates, skip, in_block, out_block, state)
                total, carry = local_states(x_block, raw_block, bias, rates, in_block)
                return (total[:, None, None] * state + carry, mixed)
            start = jnp.zeros((MAMBA_HEADS, HEAD_SIZE, STATE_SIZE), jnp.float32)
            final_state, mixed = lax.scan(jax.checkpoint(advance), start, (x_blocks, raw_blocks, in_blocks, out_blocks))
            return mixed.reshape(SEQUENCE_LENGTH, MAMBA_WIDTH)
        mamba_out, whole_back = jax.vjp(whole, mamba_in[sequence].astype(jnp.float32), step_raw[sequence], step_bias, log_rate, skip_gain, state_in[sequence].astype(jnp.float32), state_out[sequence].astype(jnp.float32))
        normed, norm_back = jax.vjp(normalize, mamba_out, norm_gain)
        drawn_numbers = normed.astype(jnp.bfloat16)
        segments, moving, slot_index = jax.vmap(doc_layout, in_axes=(0, 0, None))(doc_lengths[sequence], doc_moved[sequence], TOK_DEV)
        picks = jax.vmap(pick_mask, in_axes=(0, 0, None))(moving, slot_index, SEND_MAX).astype(jnp.float32)
        kept = moving == 0
        grads = attn_grad[sequence].reshape(N_CTX, ROWS_ATT, ATTN_WIDTH)
        returned = grads[:, TOK_DEV:][partner]
        unpacked = jnp.einsum('bst,bsd->btd', picks, returned.astype(jnp.float32), precision=HIGH).astype(jnp.bfloat16)
        grad_home = jnp.where(kept[:, :, None], grads[:, :TOK_DEV], unpacked)
        q_blocks = queries[sequence].reshape(N_CTX, TOK_DEV, ATTN_WIDTH)
        k_blocks = attn_keys[sequence].reshape(N_CTX, TOK_DEV, ATTN_WIDTH)
        v_blocks = drawn_numbers.reshape(N_CTX, TOK_DEV, ATTN_WIDTH)

        def per_block(pieces):
            q_block, k_block, v_block, seg_block, grad_block = pieces
            block_out, probs, probs_low = attend(q_block, k_block, v_block, seg_block, ATTN_HEADS)
            back = attend_back(q_block, k_block, v_block, probs, probs_low, grad_block, ATTN_HEADS)
            return (block_out,) + back
        home_out, grad_query, grad_key, grad_value = lax.map(per_block, (q_blocks, k_blocks, v_blocks, segments, grad_home))
        packed = jnp.einsum('bst,btd->bsd', picks, home_out.astype(jnp.float32), precision=HIGH).astype(jnp.bfloat16)
        layout = jnp.concatenate([jnp.where(kept[:, :, None], home_out, jnp.zeros_like(home_out)), packed[partner]], axis=1)
        out_rows_all.append(layout.reshape(N_CTX * ROWS_ATT, ATTN_WIDTH))
        gq_all.append(grad_query.reshape(SEQUENCE_LENGTH, ATTN_WIDTH))
        gk_all.append(grad_key.reshape(SEQUENCE_LENGTH, ATTN_WIDTH))
        grad_mixed, gain_part = norm_back(grad_value.reshape(SEQUENCE_LENGTH, ATTN_WIDTH).astype(jnp.float32))
        back = whole_back(grad_mixed)
        gx_all.append(back[0].astype(jnp.bfloat16))
        gstep_all.append(back[1])
        gin_all.append(back[5].astype(jnp.bfloat16))
        gout_all.append(back[6].astype(jnp.bfloat16))
        heads_total = heads_total + jnp.stack([back[3], back[2], back[4]])
        gain_total = gain_total + gain_part
    return (jnp.stack(out_rows_all), jnp.stack(gq_all), jnp.stack(gk_all), jnp.stack(gx_all), jnp.stack(gin_all), jnp.stack(gout_all), jnp.stack(gstep_all), heads_total, gain_total)
```

```python
import functools
import math

import jax
import jax.numpy as jnp
from jax import lax
from jax.experimental import pallas as pl
from jax.experimental.pallas import tpu as pltpu
from jax.sharding import PartitionSpec as P

F32 = jnp.float32
BF16 = jnp.bfloat16
HIGH = lax.Precision.HIGHEST
EPSILON = 1e-05
MASKED = -1e30

TOK = 128
HEADS = 56
SIZE = 64
GROUPS = 4
GW = 896
GH = 14
AH = 4
ASIZE = 224
WIDTH = GROUPS * GW
SEND = 64
WINDOWS = ((0, 2), (1, 3), (3, 3), (5, 2))

NT = (((1,), (1,)), ((), ()))
TN = (((0,), (0,)), ((), ()))


def dot(a, b, dims=(((1,), (0,)), ((), ())), precision=None):
    return lax.dot_general(a, b, dims, precision=precision, preferred_element_type=F32)


def iota(shape, dim):
    return lax.broadcasted_iota(jnp.int32, shape, dim)


def pad_heads(rows):
    gap = jnp.zeros((2, rows.shape[1]), rows.dtype)
    parts = []
    for g in range(GROUPS):
        parts += [rows[g * GH : (g + 1) * GH], gap]
    return jnp.concatenate(parts, axis=0)


def unpad_heads(rows):
    return jnp.concatenate([rows[16 * g : 16 * g + GH] for g in range(GROUPS)], axis=0)


def columns(*rows):
    stack = jnp.concatenate(list(rows) + [jnp.zeros((8 - len(rows), HEADS), F32)], axis=0)
    stack = jnp.concatenate([stack, jnp.zeros((8, 128 - HEADS), F32)], axis=1)
    turned = pad_heads(jnp.transpose(stack)[:HEADS])
    return [turned[:, i : i + 1] for i in range(len(rows))]


def expander(group, parts=2):
    shape = (64 * parts, GW)
    return jnp.where(
        (iota(shape, 0) & 63) == (iota(shape, 1) >> 6) + 16 * group, 1.0, 0.0
    ).astype(BF16)


def split(value):
    high = value.astype(BF16)
    low = (value - high.astype(F32)).astype(BF16)
    return high, low


def stacked_parts(value):
    high, low = split(value)
    return jnp.transpose(jnp.concatenate([high.astype(F32), low.astype(F32)], axis=0)).astype(BF16)


def decay_sums(raw, bias, rate):
    z = pad_heads(raw) + bias
    step = jnp.maximum(z, 0.0) + jnp.log1p(jnp.exp(-jnp.abs(z)))
    neg = -jnp.exp(rate)
    tri = jnp.where(iota((TOK, TOK), 0) <= iota((TOK, TOK), 1), 1.0, 0.0)
    running = dot(neg * step, tri, precision=HIGH)
    return z, step, neg, running


def lanes(g):
    return pl.ds(pl.multiple_of(g * GW, 128), GW)


def rows64(g):
    return pl.ds(pl.multiple_of(g * SIZE, SIZE), SIZE)


def states_kernel(x_ref, raw_ref, in_ref, rate_ref, bias_ref, out_ref):
    rate, bias = columns(rate_ref[...], bias_ref[...])
    _, step, _, running = decay_sums(raw_ref[...], bias, rate)
    last = running[:, TOK - 1 :]
    tail = stacked_parts(jnp.exp(last - running) * step)
    total = stacked_parts(jnp.broadcast_to(jnp.exp(last), running.shape))[:SIZE]
    turned = jnp.transpose(in_ref[...].astype(F32)).astype(BF16)
    for g in range(GROUPS):
        wide = dot(tail, expander(g))
        scaled = (x_ref[:, g * GW : (g + 1) * GW].astype(F32) * wide).astype(BF16)
        out_ref[g * SIZE : (g + 1) * SIZE, :GW] = dot(turned, scaled).astype(BF16)
        out_ref[g * SIZE : (g + 1) * SIZE, GW:] = total


def scan_kernel(blocks, reverse, carry_ref, total_ref, out_ref, wide_ref):
    group = lax.axis_index("ctx") // 8
    wide_ref[...] = dot(total_ref[:, GW:], expander(group))
    state = jnp.zeros((8, GW), F32)
    pairs = range(blocks // 2)
    for i in reversed(pairs) if reverse else pairs:
        rows = slice(16 * i, 16 * i + 16)
        carry = carry_ref[rows, :GW].astype(F32)
        first = state
        at = slice(8, 16) if reverse else slice(0, 8)
        second = wide_ref[rows][at] * first + carry[at]
        at = slice(0, 8) if reverse else slice(8, 16)
        state = wide_ref[rows][at] * second + carry[at]
        both = [second, first] if reverse else [first, second]
        out_ref[rows, :] = jnp.concatenate(both, axis=0).astype(BF16)


def lane_masks():
    masks = []
    for i, (tile, tiles) in enumerate(WINDOWS):
        at = iota((1, 128 * tiles), 1) + 128 * tile
        masks.append(jnp.where((at >= ASIZE * i) & (at < ASIZE * (i + 1)), 1.0, 0.0).astype(BF16))
    return masks


def join_windows(parts):
    tiles = [None] * 7
    for (tile, count), part in zip(WINDOWS, parts):
        for k in range(count):
            piece = part[:, 128 * k : 128 * (k + 1)]
            tiles[tile + k] = piece if tiles[tile + k] is None else tiles[tile + k] + piece
    return jnp.concatenate(tiles, axis=1)


def pair_rows(tile):
    half = jnp.where(iota((1, 128), 1) < SIZE, 1.0, 0.0).astype(BF16)
    return jnp.concatenate([tile * half, tile * (1 - half)], axis=0)


def main_kernel(
    x_ref,
    raw_ref,
    in_ref,
    out_map_ref,
    rate_ref,
    bias_ref,
    skip_ref,
    gain_ref,
    lengths_ref,
    moved_ref,
    q_ref,
    k_ref,
    grad_ref,
    back_ref,
    start_ref,
    attn_ref,
    packed_ref,
    gq_ref,
    gk_ref,
    dx_ref,
    message_ref,
    flow_ref,
    direct_ref,
    gout_ref,
    gin_ref,
    gain_sum_ref,
    skip_sum_ref,
    y_ref,
    decay_ref,
    probs_ref,
    gv_ref,
    home_ref,
    column_ref,
    row_ref,
):
    block = lax.axis_index("ctx")
    scale = 1.0 / math.sqrt(ASIZE)
    square = (TOK, TOK)
    seg_q = jnp.zeros(square, jnp.int32)
    seg_k = jnp.zeros(square, jnp.int32)
    slot_q = jnp.full(square, -1, jnp.int32)
    slot_k = jnp.full((SEND, TOK), -1, jnp.int32)
    kept = jnp.ones(square, F32)
    at_q, at_k = iota(square, 0), iota(square, 1)
    at_s = iota((SEND, TOK), 1)
    begin, sent = jnp.int32(0), jnp.int32(0)
    for d in range(8):
        length, moved = lengths_ref[0, block, d], moved_ref[0, block, d]
        end = begin + length
        seg_q += jnp.where(at_q >= end, 1, 0)
        seg_k += jnp.where(at_k >= end, 1, 0)
        limit = jnp.where(moved == 1, end, begin)
        in_q = (at_q >= begin) & (at_q < limit)
        in_s = (at_s >= begin) & (at_s < limit)
        slot_q = jnp.where(in_q, at_q + (sent - begin), slot_q)
        slot_k = jnp.where(in_s, at_s + (sent - begin), slot_k)
        kept = jnp.where(in_q, 0.0, kept)
        sent = sent + (limit - begin)
        begin = end
    allowed = (seg_q == seg_k) & (at_k <= at_q)
    pick = jnp.where(slot_k == iota((SEND, TOK), 0), 1.0, 0.0).astype(BF16)
    place = jnp.where(slot_q == at_k, 1.0, 0.0).astype(BF16)[:, :SEND]
    kept = kept.astype(BF16)[:, :1]
    masks = lane_masks()

    rate, bias, skip = columns(rate_ref[...], bias_ref[...], skip_ref[...])
    _, step, _, running = decay_sums(raw_ref[...], bias, rate)
    grown = stacked_parts(jnp.exp(running))
    skips = stacked_parts(jnp.broadcast_to(skip, (SIZE, TOK)))[:16]
    row_ref[...] = running - jnp.log(step)
    column = jnp.transpose(jnp.concatenate([running, running], axis=0))
    for g in range(GROUPS):
        column_ref[g] = pltpu.roll(column, 128 - 16 * g, 1) if g else column
    in_rows, out_rows = in_ref[...], out_map_ref[...]
    gram = jnp.where(at_q >= at_k, dot(out_rows, in_rows, NT), 0.0)

    def forward(g, sums):
        power, along = sums
        at = lanes(g)
        x = x_ref[:, at]
        grad = grad_ref[0:TOK, at] * kept + dot(place, back_ref[:, at]).astype(BF16)
        home_ref[:, at] = grad
        q, k = q_ref[:, at], k_ref[:, at]
        parts = []
        for i, (tile, count) in enumerate(WINDOWS):
            window = slice(128 * tile, 128 * (tile + count))
            scores = dot(q[:, window] * masks[i], k[:, window], NT) * scale
            scores = jnp.where(allowed, scores, MASKED)
            weights = jnp.exp(scores - jnp.max(scores, axis=-1, keepdims=True))
            probs = weights * (1.0 / jnp.sum(weights, axis=-1, keepdims=True))
            probs_ref[AH * g + i] = probs
            parts.append(dot(probs.astype(BF16), grad[:, window] * masks[i], TN))
        gv = join_windows(parts).astype(BF16)
        gv_ref[:, at] = gv
        wide = expander(g)
        y = dot(out_rows, start_ref[rows64(g), :]) * dot(grown, wide)
        y = y + dot(skips, wide)[:1] * x.astype(F32)
        heads = row_ref[pl.ds(pl.multiple_of(16 * g, 16), 16), :]
        column = column_ref[g]
        inner = []
        for i in range(GH // 2):
            mixing = []
            for h in (2 * i, 2 * i + 1):
                decay = jnp.exp(jnp.minimum(column[:, h : h + 1] - heads[h : h + 1], 20.0))
                decay_ref[GH * g + h] = decay
                mixing.append((decay * gram).astype(BF16))
            pair = pair_rows(x[:, 128 * i : 128 * (i + 1)])
            inner.append(dot(jnp.concatenate(mixing, axis=1), pair))
        y = y + jnp.concatenate(inner, axis=1)
        y_ref[:, at] = y
        scaled = gv.astype(F32) * gain_ref[:, at]
        power = power + jnp.sum(y * y, axis=-1, keepdims=True)
        along = along + jnp.sum(scaled * y, axis=-1, keepdims=True)
        return power, along

    zero = jnp.zeros((TOK, 1), F32)
    power, along = lax.fori_loop(0, GROUPS, forward, (zero, zero))
    inverse = lax.rsqrt(power * (1.0 / WIDTH) + EPSILON)
    slope = inverse * inverse * inverse * along * (1.0 / WIDTH)

    gout_ref[...] = jnp.zeros_like(gout_ref)
    flow_ref[...] = jnp.zeros_like(flow_ref)
    direct_ref[...] = jnp.zeros_like(direct_ref)
    turned = jnp.transpose(out_rows.astype(F32)).astype(BF16)

    def backward(g, carry):
        gram_grad, skip_sum = carry
        at = lanes(g)
        x, y = x_ref[:, at], y_ref[:, at]
        gain = gain_ref[:, at]
        gv = gv_ref[:, at].astype(F32)
        normed = y * inverse
        values = (normed * gain).astype(BF16)
        gain_sum_ref[:, at] = jnp.sum(gv * normed, axis=0, keepdims=True)
        mixed_grad = gv * gain * inverse - y * slope
        low_grad = mixed_grad.astype(BF16)
        q, k, grad = q_ref[:, at], k_ref[:, at], home_ref[:, at]
        outs, gqs, gks = [], [], []
        for i, (tile, count) in enumerate(WINDOWS):
            window = slice(128 * tile, 128 * (tile + count))
            probs = probs_ref[AH * g + i]
            vals = values[:, window] * masks[i]
            outs.append(dot(probs.astype(BF16), vals))
            dprobs = dot(grad[:, window], vals, NT)
            delta = jnp.sum(probs * dprobs, axis=-1, keepdims=True)
            dscores = (probs * (dprobs - delta) * scale).astype(BF16)
            gqs.append(dot(dscores, k[:, window] * masks[i]))
            gks.append(dot(dscores, q[:, window] * masks[i], TN))
        head_out = join_windows(outs).astype(BF16)
        attn_ref[0:TOK, at] = head_out * kept
        packed_ref[:, at] = dot(pick, head_out).astype(BF16)
        gq_ref[:, at] = join_windows(gqs).astype(BF16)
        gk_ref[:, at] = join_windows(gks).astype(BF16)
        wide = expander(g)
        grown_grad = (dot(grown, wide) * mixed_grad).astype(BF16)
        message_ref[rows64(g), :] = dot(turned, grown_grad).astype(BF16)
        gout_ref[...] += dot(grown_grad, start_ref[rows64(g), :], NT)
        inner = []
        for i in range(GH // 2):
            tile = slice(128 * i, 128 * (i + 1))
            both = dot(low_grad[:, tile], pair_rows(x[:, tile]), NT)
            mixing = []
            for j in (0, 1):
                decay = decay_ref[GH * g + 2 * i + j]
                gram_grad = gram_grad + both[:, TOK * j : TOK * (j + 1)] * decay
                mixing.append((decay * gram).astype(BF16))
            inner.append(dot(jnp.concatenate(mixing, axis=0), pair_rows(low_grad[:, tile]), TN))
        inner = jnp.concatenate(inner, axis=1)
        wide_skip = dot(skips, wide)[:1]
        x = x.astype(F32)
        dx_ref[:, at] = inner + wide_skip * mixed_grad
        product = x * inner
        high, low = split(low_grad.astype(F32) * (y - wide_skip * x) - product)
        seg = expander(g)
        flow_ref[...] += dot(high, seg, NT) + dot(low, seg, NT)
        high, low = split(product)
        direct_ref[...] += dot(high, seg, NT) + dot(low, seg, NT)
        high, low = split(jnp.broadcast_to(jnp.sum(mixed_grad * x, axis=0, keepdims=True), (16, GW)))
        skip_sum = skip_sum + dot(high, seg, NT) + dot(low, seg, NT)
        return gram_grad, skip_sum

    gram_grad, skip_sum = lax.fori_loop(
        0, GROUPS, backward, (jnp.zeros(square, F32), jnp.zeros((16, TOK), F32))
    )
    skip_sum_ref[...] = skip_sum[:1]
    gram_grad = jnp.where(at_q >= at_k, gram_grad, 0.0).astype(BF16)
    gout_ref[...] += dot(gram_grad, in_rows)
    gin_ref[...] = dot(gram_grad, out_rows, TN)


def late_kernel(
    x_ref,
    raw_ref,
    in_ref,
    rate_ref,
    bias_ref,
    start_ref,
    grad_ref,
    dx_ref,
    flow_ref,
    direct_ref,
    gin_ref,
    arrived_ref,
    attn_in_ref,
    gx_ref,
    gin_out_ref,
    step_ref,
    heads_ref,
    attn_ref,
    sem,
):
    del attn_in_ref
    copy = pltpu.make_async_copy(arrived_ref, attn_ref.at[pl.ds(TOK, SEND), :], sem)
    copy.start()
    rate, bias = columns(rate_ref[...], bias_ref[...])
    z, step, neg, running = decay_sums(raw_ref[...], bias, rate)
    last = running[:, TOK - 1 :]
    tail = stacked_parts(jnp.exp(last - running) * step)
    in_rows = in_ref[...]
    tail_sum = jnp.zeros((TOK, TOK), F32)
    overlap = jnp.zeros((16, TOK), F32)
    gin = gin_ref[...]
    for g in range(GROUPS):
        at = slice(g * GW, (g + 1) * GW)
        rows = slice(g * SIZE, (g + 1) * SIZE)
        grad = grad_ref[rows, :]
        wide = expander(g)
        weight = dot(tail, wide)
        x = x_ref[:, at].astype(F32)
        late = dot(in_rows, grad) * weight
        gx_ref[:, at] = (dx_ref[:, at] + late).astype(BF16)
        gin = gin + dot((x * weight).astype(BF16), grad, NT)
        high, low = split(x * late)
        tail_sum = tail_sum + dot(high, wide, NT) + dot(low, wide, NT)
        both = jnp.sum(start_ref[rows, :].astype(F32) * grad.astype(F32), axis=0, keepdims=True)
        high, low = split(jnp.broadcast_to(both, (16, GW)))
        overlap = overlap + dot(high, wide, NT) + dot(low, wide, NT)
    gin_out_ref[...] = gin.astype(BF16)
    tail_sum = jnp.transpose(tail_sum)[:SIZE]
    flow = jnp.transpose(flow_ref[...])[:SIZE]
    direct = jnp.transpose(direct_ref[...])[:SIZE]
    overlap = jnp.transpose(jnp.broadcast_to(overlap[:1], (TOK, TOK)))[:SIZE]
    tri = jnp.where(iota((TOK, TOK), 0) >= iota((TOK, TOK), 1), 1.0, 0.0)
    ahead = dot(flow - tail_sum, tri, precision=HIGH)
    ahead = ahead + jnp.sum(tail_sum, axis=1, keepdims=True) + jnp.exp(last) * overlap
    step_grad = (direct + tail_sum) / step + neg * ahead
    raw_grad = step_grad * (1.0 / (1.0 + jnp.exp(-z)))
    step_ref[...] = unpad_heads(raw_grad)
    rate_grad = jnp.sum(neg * step * ahead, axis=1, keepdims=True)
    bias_grad = jnp.sum(raw_grad, axis=1, keepdims=True)
    both = jnp.concatenate([rate_grad, bias_grad], axis=0)
    heads_ref[:, 0, :] = jnp.transpose(jnp.broadcast_to(both, (TOK, TOK)))
    copy.wait()


def vmem(count):
    return [pl.BlockSpec(memory_space=pltpu.VMEM)] * count


PARAMS = pltpu.CompilerParams(vmem_limit_bytes=56 * 1024 * 1024)


def shape(dims, dtype):
    return jax.ShapeDtypeStruct(dims, dtype)


def local(
    mamba_in,
    step_raw,
    state_in,
    state_out,
    log_rate,
    step_bias,
    skip_gain,
    norm_gain,
    doc_lengths,
    doc_moved,
    queries,
    attn_keys,
    attn_grad,
):
    x, raw, in_rows, out_rows = mamba_in[0], step_raw[0], state_in[0], state_out[0]
    rate, bias, skip = log_rate[None], step_bias[None], skip_gain[None]
    blocks = lax.axis_size("ctx")
    devices = blocks * lax.axis_size("dp")
    rows = 8 * blocks
    swap = [(i, i ^ (blocks // 2)) for i in range(blocks)]

    def exchange(value):
        value = value.reshape(blocks, 8, value.shape[1])
        value = lax.all_to_all(value, "ctx", 0, 0, tiled=True)
        return value.reshape(rows, value.shape[2])

    def scan(reverse, carry, total):
        return pl.pallas_call(
            functools.partial(scan_kernel, blocks, reverse),
            out_shape=shape((rows, GW), BF16),
            in_specs=vmem(2),
            out_specs=pl.BlockSpec(memory_space=pltpu.VMEM),
            scratch_shapes=[pltpu.VMEM((rows, GW), F32)],
            compiler_params=PARAMS,
        )(carry, total)

    back = lax.ppermute(attn_grad[0, TOK:], "ctx", swap)
    message = pl.pallas_call(
        states_kernel,
        out_shape=shape((rows, GW + 128), BF16),
        in_specs=vmem(5),
        out_specs=pl.BlockSpec(memory_space=pltpu.VMEM),
        compiler_params=PARAMS,
    )(x, raw, in_rows, rate, bias)
    gathered = exchange(message)
    start = exchange(scan(False, gathered, gathered))

    outs = pl.pallas_call(
        main_kernel,
        out_shape=(
            shape((TOK + SEND, WIDTH), BF16),
            shape((SEND, WIDTH), BF16),
            shape((TOK, WIDTH), BF16),
            shape((TOK, WIDTH), BF16),
            shape((TOK, WIDTH), F32),
            shape((rows, GW), BF16),
            shape((TOK, TOK), F32),
            shape((TOK, TOK), F32),
            shape((TOK, SIZE), F32),
            shape((TOK, SIZE), F32),
            shape((1, WIDTH), F32),
            shape((1, TOK), F32),
        ),
        in_specs=vmem(8) + [pl.BlockSpec(memory_space=pltpu.SMEM)] * 2 + vmem(5),
        out_specs=tuple(vmem(12)),
        scratch_shapes=[
            pltpu.VMEM((TOK, WIDTH), F32),
            pltpu.VMEM((HEADS, TOK, TOK), F32),
            pltpu.VMEM((GROUPS * AH, TOK, TOK), F32),
            pltpu.VMEM((TOK, WIDTH), BF16),
            pltpu.VMEM((TOK, WIDTH), BF16),
            pltpu.VMEM((GROUPS, TOK, TOK), F32),
            pltpu.VMEM((SIZE, TOK), F32),
        ],
        compiler_params=PARAMS,
    )(
        x,
        raw,
        in_rows,
        out_rows,
        rate,
        bias,
        skip,
        norm_gain[None],
        doc_lengths,
        doc_moved,
        queries[0],
        attn_keys[0],
        attn_grad[0],
        back,
        start,
    )
    attn, packed, gq, gk, dx, message, flow, direct, gout, gin, gain_part, skip_part = outs
    arrived = lax.ppermute(packed, "ctx", swap)
    gain_sum, skip_sum = lax.psum((gain_part[0], skip_part[0]), ("dp", "ctx"))
    state_grad = exchange(scan(True, exchange(message), gathered))

    hbm = pl.BlockSpec(memory_space=pl.ANY)
    gx, gin, gstep, heads, attn = pl.pallas_call(
        late_kernel,
        out_shape=(
            shape((TOK, WIDTH), BF16),
            shape((TOK, SIZE), BF16),
            shape((HEADS, TOK), F32),
            shape((devices, 1, TOK), F32),
            shape((TOK + SEND, WIDTH), BF16),
        ),
        in_specs=vmem(11) + [hbm, hbm],
        out_specs=tuple(vmem(4)) + (hbm,),
        scratch_shapes=[pltpu.SemaphoreType.DMA],
        input_output_aliases={12: 4},
        compiler_params=PARAMS,
    )(x, raw, in_rows, rate, bias, start, state_grad, dx, flow, direct, gin, arrived, attn)
    heads = lax.all_to_all(heads, ("dp", "ctx"), 0, 0, tiled=True)
    heads = jnp.sum(heads, axis=(0, 1))
    head_sum = jnp.concatenate([heads.reshape(2, SIZE), skip_sum[None, :SIZE]], axis=0)
    head_sum = head_sum.reshape(3, GROUPS, 16)[:, :, :GH].reshape(3, HEADS)
    return (
        attn[None],
        gq[None],
        gk[None],
        gx[None],
        gin[None],
        gout.astype(BF16)[None],
        gstep[None],
        head_sum,
        gain_sum,
    )


def solution(mesh):
    in_specs = (
        P("dp", "ctx", None),
        P("dp", None, "ctx"),
        P("dp", "ctx", None),
        P("dp", "ctx", None),
        P(),
        P(),
        P(),
        P(),
        P("dp", None, None),
        P("dp", None, None),
        P("dp", "ctx", None),
        P("dp", "ctx", None),
        P("dp", "ctx", None),
    )
    out_specs = (
        P("dp", "ctx", None),
        P("dp", "ctx", None),
        P("dp", "ctx", None),
        P("dp", "ctx", None),
        P("dp", "ctx", None),
        P("dp", "ctx", None),
        P("dp", None, "ctx"),
        P(),
        P(),
    )
    return jax.shard_map(local, mesh=mesh, in_specs=in_specs, out_specs=out_specs, check_vma=False)
```

```python
import functools
import math

import jax
import jax.numpy as jnp
from jax import lax
from jax.experimental import pallas as pl
from jax.experimental.pallas import tpu as pltpu
from jax.sharding import PartitionSpec as P

F32 = jnp.float32
BF16 = jnp.bfloat16
HIGH = lax.Precision.HIGHEST
EPSILON = 1e-05
MASKED = -1e30

TOK = 128
HEADS = 56
SIZE = 64
GROUPS = 4
GW = 896
GH = 14
AH = 4
ASIZE = 224
WIDTH = GROUPS * GW
SEND = 64
WINDOWS = ((0, 2), (1, 3), (3, 3), (5, 2))

NT = (((1,), (1,)), ((), ()))
TN = (((0,), (0,)), ((), ()))


def dot(a, b, dims=(((1,), (0,)), ((), ())), precision=None):
    return lax.dot_general(a, b, dims, precision=precision, preferred_element_type=F32)


def iota(shape, dim):
    return lax.broadcasted_iota(jnp.int32, shape, dim)


def pad_heads(rows):
    gap = jnp.zeros((2, rows.shape[1]), rows.dtype)
    parts = []
    for g in range(GROUPS):
        parts += [rows[g * GH : (g + 1) * GH], gap]
    return jnp.concatenate(parts, axis=0)


def unpad_heads(rows):
    return jnp.concatenate([rows[16 * g : 16 * g + GH] for g in range(GROUPS)], axis=0)


def columns(*rows):
    stack = jnp.concatenate(list(rows) + [jnp.zeros((8 - len(rows), HEADS), F32)], axis=0)
    stack = jnp.concatenate([stack, jnp.zeros((8, 128 - HEADS), F32)], axis=1)
    turned = pad_heads(jnp.transpose(stack)[:HEADS])
    return [turned[:, i : i + 1] for i in range(len(rows))]


def expander(group, parts=2):
    shape = (64 * parts, GW)
    return jnp.where(
        (iota(shape, 0) & 63) == (iota(shape, 1) >> 6) + 16 * group, 1.0, 0.0
    ).astype(BF16)


def split(value):
    high = value.astype(BF16)
    low = (value - high.astype(F32)).astype(BF16)
    return high, low


def stacked_parts(value):
    high, low = split(value)
    return jnp.transpose(jnp.concatenate([high.astype(F32), low.astype(F32)], axis=0)).astype(BF16)


def decay_sums(raw, bias, rate):
    z = pad_heads(raw) + bias
    step = jnp.maximum(z, 0.0) + jnp.log1p(jnp.exp(-jnp.abs(z)))
    neg = -jnp.exp(rate)
    tri = jnp.where(iota((TOK, TOK), 0) <= iota((TOK, TOK), 1), 1.0, 0.0)
    running = dot(neg * step, tri, precision=HIGH)
    return z, step, neg, running


def lanes(g):
    return pl.ds(pl.multiple_of(g * GW, 128), GW)


def rows64(g):
    return pl.ds(pl.multiple_of(g * SIZE, SIZE), SIZE)


def states_kernel(x_ref, raw_ref, in_ref, rate_ref, bias_ref, out_ref):
    rate, bias = columns(rate_ref[...], bias_ref[...])
    _, step, _, running = decay_sums(raw_ref[...], bias, rate)
    last = running[:, TOK - 1 :]
    tail = stacked_parts(jnp.exp(last - running) * step)
    total = stacked_parts(jnp.broadcast_to(jnp.exp(last), running.shape))[:SIZE]
    in_map = in_ref[...]
    for g in range(GROUPS):
        wide = dot(tail, expander(g))
        scaled = (x_ref[:, g * GW : (g + 1) * GW].astype(F32) * wide).astype(BF16)
        out_ref[g * SIZE : (g + 1) * SIZE, :GW] = dot(in_map, scaled).astype(BF16)
        out_ref[g * SIZE : (g + 1) * SIZE, GW:] = total


def scan_kernel(blocks, reverse, *refs):
    if reverse:
        carry_ref, total_ref, out_ref, sum_ref, wide_ref = refs
        ones = jnp.ones((16, 8 * blocks), BF16)
        sum_ref[...] = dot(ones, carry_ref[:, GW:])[:1]
    else:
        carry_ref, out_ref, wide_ref = refs
        total_ref = carry_ref
    group = lax.axis_index("ctx") // 8
    wide_ref[...] = dot(total_ref[:, GW:], expander(group))
    state = jnp.zeros((8, GW), F32)
    pairs = range(blocks // 2)
    for i in reversed(pairs) if reverse else pairs:
        rows = slice(16 * i, 16 * i + 16)
        carry = carry_ref[rows, :GW].astype(F32)
        first = state
        at = slice(8, 16) if reverse else slice(0, 8)
        second = wide_ref[rows][at] * first + carry[at]
        at = slice(0, 8) if reverse else slice(8, 16)
        state = wide_ref[rows][at] * second + carry[at]
        both = [second, first] if reverse else [first, second]
        out_ref[rows, :] = jnp.concatenate(both, axis=0).astype(BF16)


def lane_masks():
    masks = []
    for i, (tile, tiles) in enumerate(WINDOWS):
        at = iota((1, 128 * tiles), 1) + 128 * tile
        masks.append(jnp.where((at >= ASIZE * i) & (at < ASIZE * (i + 1)), 1.0, 0.0).astype(BF16))
    return masks


def join_windows(parts):
    tiles = [None] * 7
    for (tile, count), part in zip(WINDOWS, parts):
        for k in range(count):
            piece = part[:, 128 * k : 128 * (k + 1)]
            tiles[tile + k] = piece if tiles[tile + k] is None else tiles[tile + k] + piece
    return jnp.concatenate(tiles, axis=1)


def pair_rows(tile):
    half = jnp.where(iota((1, 128), 1) < SIZE, 1.0, 0.0).astype(BF16)
    return jnp.concatenate([tile * half, tile * (1 - half)], axis=0)


def documents(lengths_ref, moved_ref):
    block = lax.axis_index("ctx")
    begin, sent, docs = jnp.int32(0), jnp.int32(0), []
    for d in range(8):
        length, moved = lengths_ref[d, block], moved_ref[d, block]
        end = begin + length
        limit = jnp.where(moved == 1, end, begin)
        docs.append((begin, end, limit, sent))
        sent = sent + (limit - begin)
        begin = end
    return docs


def place_slots(docs, dims, dim):
    at = iota(dims, dim)
    slots = jnp.full(dims, -1, jnp.int32)
    for begin, _, limit, sent in docs:
        slots = jnp.where((at >= begin) & (at < limit), at + (sent - begin), slots)
    return slots


def columns_of(running):
    turned = jnp.transpose(jnp.concatenate([running, running], axis=0))
    return [turned] + [pltpu.roll(turned, TOK - 16 * g, 1) for g in range(1, GROUPS)]


def local_decay(column, heads, h):
    return jnp.exp(jnp.minimum(column[:, h : h + 1] - heads[h : h + 1], 20.0))


def inner_kernel(
    x_ref,
    raw_ref,
    in_ref,
    map_ref,
    rate_ref,
    bias_ref,
    skip_ref,
    lengths_ref,
    moved_ref,
    q_ref,
    k_ref,
    y_ref,
    probs_ref,
    column_ref,
    row_ref,
):
    scale = 1.0 / math.sqrt(ASIZE)
    square = (TOK, TOK)
    at_q, at_k = iota(square, 0), iota(square, 1)
    docs = documents(lengths_ref, moved_ref)
    seg_q = jnp.zeros(square, jnp.int32)
    seg_k = jnp.zeros(square, jnp.int32)
    for _, end, _, _ in docs:
        seg_q += jnp.where(at_q >= end, 1, 0)
        seg_k += jnp.where(at_k >= end, 1, 0)
    allowed = (seg_q == seg_k) & (at_k <= at_q)
    masks = lane_masks()
    rate, bias, skip = columns(rate_ref[...], bias_ref[...], skip_ref[...])
    _, step, _, running = decay_sums(raw_ref[...], bias, rate)
    skips = stacked_parts(jnp.broadcast_to(skip, (SIZE, TOK)))[:16]
    row_ref[...] = running - jnp.log(step)
    for g, column in enumerate(columns_of(running)):
        column_ref[g] = column
    gram = jnp.where(at_q >= at_k, dot(map_ref[...], in_ref[...], TN), 0.0)

    def group(g, carry):
        at = lanes(g)
        x, q, k = x_ref[:, at], q_ref[:, at], k_ref[:, at]
        for i, (tile, count) in enumerate(WINDOWS):
            window = slice(128 * tile, 128 * (tile + count))
            scores = dot(q[:, window] * masks[i], k[:, window], NT) * scale
            scores = jnp.where(allowed, scores, MASKED)
            weights = jnp.exp(scores - jnp.max(scores, axis=-1, keepdims=True))
            total = jnp.sum(weights, axis=-1, keepdims=True)
            probs_ref[AH * g + i] = weights * (1.0 / total)
        heads = row_ref[pl.ds(pl.multiple_of(16 * g, 16), 16), :]
        column = column_ref[g]
        inner = []
        for i in range(GH // 2):
            pair = [(local_decay(column, heads, h) * gram).astype(BF16) for h in (2 * i, 2 * i + 1)]
            rows = pair_rows(x[:, 128 * i : 128 * (i + 1)])
            inner.append(dot(jnp.concatenate(pair, axis=1), rows))
        y_ref[:, at] = jnp.concatenate(inner, axis=1) + dot(skips, expander(g))[:1] * x.astype(F32)
        return carry

    lax.fori_loop(0, GROUPS, group, 0)


def value_grad_kernel(lengths_ref, moved_ref, probs_ref, grad_ref, back_ref, gv_ref, home_ref):
    docs = documents(lengths_ref, moved_ref)
    slots = place_slots(docs, (TOK, TOK), 0)
    place = jnp.where(slots == iota((TOK, TOK), 1), 1.0, 0.0).astype(BF16)[:, :SEND]
    kept = jnp.where(slots < 0, 1.0, 0.0).astype(BF16)[:, :1]
    masks = lane_masks()

    def group(g, carry):
        at = lanes(g)
        grad = grad_ref[0:TOK, at] * kept + dot(place, back_ref[:, at]).astype(BF16)
        home_ref[:, at] = grad
        parts = []
        for i, (tile, count) in enumerate(WINDOWS):
            window = slice(128 * tile, 128 * (tile + count))
            parts.append(dot(probs_ref[AH * g + i].astype(BF16), grad[:, window] * masks[i], TN))
        gv_ref[:, at] = join_windows(parts).astype(BF16)
        return carry

    lax.fori_loop(0, GROUPS, group, 0)


def norm_kernel(
    raw_ref,
    map_ref,
    rate_ref,
    bias_ref,
    gain_ref,
    start_ref,
    inner_ref,
    gv_ref,
    y_ref,
    values_ref,
    low_ref,
    message_ref,
    wide_ref,
    sums_ref,
):
    rate, bias = columns(rate_ref[...], bias_ref[...])
    _, _, _, running = decay_sums(raw_ref[...], bias, rate)
    grown = stacked_parts(jnp.exp(running))
    map_in = map_ref[...]
    out_rows = jnp.transpose(map_in.astype(F32)).astype(BF16)
    power = jnp.zeros((TOK, 1), F32)
    along = jnp.zeros((TOK, 1), F32)
    for g in range(GROUPS):
        at = slice(g * GW, (g + 1) * GW)
        wide = dot(grown, expander(g))
        wide_ref[:, at] = wide
        y = inner_ref[:, at] + dot(out_rows, start_ref[g * SIZE : (g + 1) * SIZE, :]) * wide
        y_ref[:, at] = y
        power = power + jnp.sum(y * y, axis=-1, keepdims=True)
        scaled = gv_ref[:, at].astype(F32) * gain_ref[:, at]
        along = along + jnp.sum(scaled * y, axis=-1, keepdims=True)
    inverse = lax.rsqrt(power * (1.0 / WIDTH) + EPSILON)
    slope = inverse * inverse * inverse * along * (1.0 / WIDTH)
    sums_ref[...] = jnp.zeros_like(sums_ref)
    for g in range(GROUPS):
        at = slice(g * GW, (g + 1) * GW)
        rows = slice(g * SIZE, (g + 1) * SIZE)
        y, gain, gv = y_ref[:, at], gain_ref[:, at], gv_ref[:, at].astype(F32)
        normed = y * inverse
        values_ref[:, at] = (normed * gain).astype(BF16)
        gain_sum = jnp.sum(gv * normed, axis=0, keepdims=True)
        for i in range(7):
            sums_ref[7 * g + i : 7 * g + i + 1, :] = gain_sum[:, 128 * i : 128 * (i + 1)]
        mixed_grad = gv * gain * inverse - y * slope
        low_ref[:, at] = mixed_grad.astype(BF16)
        grown_grad = (wide_ref[:, at] * mixed_grad).astype(BF16)
        message_ref[rows, :GW] = dot(map_in, grown_grad).astype(BF16)
    sums = sums_ref[...]
    high, low = split(sums)
    lowest = (sums - high.astype(F32) - low.astype(F32)).astype(BF16)
    dims = (message_ref.shape[0], 96)
    at, source = iota(dims, 0), iota(dims, 1)
    spread = jnp.where((at >> 3 == source & 31) & (at & 7 == source >> 5), 1.0, 0.0).astype(BF16)
    message_ref[:, GW:] = dot(spread, jnp.concatenate([high, low, lowest], axis=0)).astype(BF16)


def attention_kernel(
    lengths_ref,
    moved_ref,
    q_ref,
    k_ref,
    values_ref,
    probs_ref,
    home_ref,
    attn_ref,
    packed_ref,
    gq_ref,
    gk_ref,
):
    scale = 1.0 / math.sqrt(ASIZE)
    docs = documents(lengths_ref, moved_ref)
    pick = place_slots(docs, (SEND, TOK), 1) == iota((SEND, TOK), 0)
    pick = jnp.where(pick, 1.0, 0.0).astype(BF16)
    kept = jnp.where(place_slots(docs, (TOK, TOK), 0) < 0, 1.0, 0.0).astype(BF16)[:, :1]
    masks = lane_masks()

    def group(g, carry):
        at = lanes(g)
        q, k, grad, values = q_ref[:, at], k_ref[:, at], home_ref[:, at], values_ref[:, at]
        outs, gqs, gks = [], [], []
        for i, (tile, count) in enumerate(WINDOWS):
            window = slice(128 * tile, 128 * (tile + count))
            probs = probs_ref[AH * g + i]
            vals = values[:, window] * masks[i]
            outs.append(dot(probs.astype(BF16), vals))
            dprobs = dot(grad[:, window], vals, NT)
            delta = jnp.sum(probs * dprobs, axis=-1, keepdims=True)
            dscores = (probs * (dprobs - delta) * scale).astype(BF16)
            gqs.append(dot(dscores, k[:, window] * masks[i]))
            gks.append(dot(dscores, q[:, window] * masks[i], TN))
        head_out = join_windows(outs).astype(BF16)
        attn_ref[0:TOK, at] = head_out * kept
        packed_ref[:, at] = dot(pick, head_out).astype(BF16)
        gq_ref[:, at] = join_windows(gqs).astype(BF16)
        gk_ref[:, at] = join_windows(gks).astype(BF16)
        return carry

    lax.fori_loop(0, GROUPS, group, 0)


def inner_back_kernel(
    x_ref,
    raw_ref,
    in_ref,
    map_ref,
    rate_ref,
    bias_ref,
    skip_ref,
    start_ref,
    y_ref,
    low_ref,
    dx_ref,
    flow_ref,
    direct_ref,
    gout_ref,
    gin_ref,
    skip_sum_ref,
    column_ref,
    row_ref,
    sum_ref,
):
    square = (TOK, TOK)
    causal = iota(square, 0) >= iota(square, 1)
    rate, bias, skip = columns(rate_ref[...], bias_ref[...], skip_ref[...])
    _, step, _, running = decay_sums(raw_ref[...], bias, rate)
    skips = stacked_parts(jnp.broadcast_to(skip, (SIZE, TOK)))[:16]
    grown = stacked_parts(jnp.exp(running))
    row_ref[...] = running - jnp.log(step)
    for g, column in enumerate(columns_of(running)):
        column_ref[g] = column
    in_map, map_in = in_ref[...], map_ref[...]
    gram = jnp.where(causal, dot(map_in, in_map, TN), 0.0)
    flow_ref[...] = jnp.zeros_like(flow_ref)
    direct_ref[...] = jnp.zeros_like(direct_ref)
    sum_ref[...] = jnp.zeros_like(sum_ref)

    def group(g, carry):
        gram_grad, skip_sum = carry
        at = lanes(g)
        x, low_grad = x_ref[:, at], low_ref[:, at]
        mixed_grad = low_grad.astype(F32)
        wide = expander(g)
        grown_grad = (dot(grown, wide) * mixed_grad).astype(BF16)
        sum_ref[...] += dot(start_ref[rows64(g), :], grown_grad, NT)
        heads = row_ref[pl.ds(pl.multiple_of(16 * g, 16), 16), :]
        column = column_ref[g]
        inner = []
        for i in range(GH // 2):
            tile = slice(128 * i, 128 * (i + 1))
            both = dot(low_grad[:, tile], pair_rows(x[:, tile]), NT)
            pair = []
            for j in (0, 1):
                decay = local_decay(column, heads, 2 * i + j)
                gram_grad = gram_grad + both[:, TOK * j : TOK * (j + 1)] * decay
                pair.append((decay * gram).astype(BF16))
            inner.append(dot(jnp.concatenate(pair, axis=0), pair_rows(low_grad[:, tile]), TN))
        inner = jnp.concatenate(inner, axis=1)
        wide_skip = dot(skips, wide)[:1]
        x = x.astype(F32)
        dx_ref[:, at] = inner + wide_skip * mixed_grad
        product = x * inner
        high, low = split(mixed_grad * (y_ref[:, at] - wide_skip * x) - product)
        flow_ref[...] += dot(high, wide, NT) + dot(low, wide, NT)
        high, low = split(product)
        direct_ref[...] += dot(high, wide, NT) + dot(low, wide, NT)
        high, low = split(jnp.broadcast_to(jnp.sum(mixed_grad * x, axis=0, keepdims=True), (16, GW)))
        skip_sum = skip_sum + dot(high, wide, NT) + dot(low, wide, NT)
        return gram_grad, skip_sum

    gram_grad, skip_sum = lax.fori_loop(
        0, GROUPS, group, (jnp.zeros(square, F32), jnp.zeros((16, TOK), F32))
    )
    skip_sum_ref[...] = skip_sum[:1]
    gram_grad = jnp.where(causal, gram_grad, 0.0).astype(BF16)
    gout_ref[...] = (sum_ref[...] + dot(in_map, gram_grad, NT)).astype(BF16)
    gin_ref[...] = dot(map_in, gram_grad)


def late_kernel(
    x_ref,
    raw_ref,
    in_ref,
    rate_ref,
    bias_ref,
    start_ref,
    grad_ref,
    dx_ref,
    flow_ref,
    direct_ref,
    gin_ref,
    skip_sum_ref,
    gain_sum_ref,
    gx_ref,
    gin_out_ref,
    step_ref,
    sums_ref,
):
    rate, bias = columns(rate_ref[...], bias_ref[...])
    z, step, neg, running = decay_sums(raw_ref[...], bias, rate)
    last = running[:, TOK - 1 :]
    tail = stacked_parts(jnp.exp(last - running) * step)
    in_rows = jnp.transpose(in_ref[...].astype(F32)).astype(BF16)
    tail_sum = jnp.zeros((TOK, TOK), F32)
    overlap = jnp.zeros((16, TOK), F32)
    gin = gin_ref[...]
    for g in range(GROUPS):
        at = slice(g * GW, (g + 1) * GW)
        rows = slice(g * SIZE, (g + 1) * SIZE)
        grad = grad_ref[rows, :]
        wide = expander(g)
        weight = dot(tail, wide)
        x = x_ref[:, at].astype(F32)
        late = dot(in_rows, grad) * weight
        gx_ref[:, at] = (dx_ref[:, at] + late).astype(BF16)
        gin = gin + dot(grad, (x * weight).astype(BF16), NT)
        high, low = split(x * late)
        tail_sum = tail_sum + dot(high, wide, NT) + dot(low, wide, NT)
        both = jnp.sum(start_ref[rows, :].astype(F32) * grad.astype(F32), axis=0, keepdims=True)
        high, low = split(jnp.broadcast_to(both, (16, GW)))
        overlap = overlap + dot(high, wide, NT) + dot(low, wide, NT)
    gin_out_ref[...] = gin.astype(BF16)
    tail_sum = jnp.transpose(tail_sum)[:SIZE]
    flow = jnp.transpose(flow_ref[...])[:SIZE]
    direct = jnp.transpose(direct_ref[...])[:SIZE]
    overlap = jnp.transpose(jnp.broadcast_to(overlap[:1], (TOK, TOK)))[:SIZE]
    tri = jnp.where(iota((TOK, TOK), 0) >= iota((TOK, TOK), 1), 1.0, 0.0)
    ahead = dot(flow - tail_sum, tri, precision=HIGH)
    ahead = ahead + jnp.sum(tail_sum, axis=1, keepdims=True) + jnp.exp(last) * overlap
    step_grad = (direct + tail_sum) / step + neg * ahead
    raw_grad = step_grad * (1.0 / (1.0 + jnp.exp(-z)))
    step_ref[...] = unpad_heads(raw_grad)
    rate_grad = jnp.sum(neg * step * ahead, axis=1, keepdims=True)
    bias_grad = jnp.sum(raw_grad, axis=1, keepdims=True)
    both = jnp.concatenate([rate_grad, bias_grad], axis=0)
    devices = sums_ref.shape[0]
    sums_ref[:, 0, 0:TOK] = jnp.transpose(jnp.broadcast_to(both, (TOK, TOK)))[:devices]
    sums_ref[:, 0, TOK : 2 * TOK] = jnp.broadcast_to(skip_sum_ref[...], (devices, TOK))
    sums_ref[:, 0, 2 * TOK :] = jnp.broadcast_to(gain_sum_ref[...], (devices, TOK))


def last_kernel(blocks, sums_ref, heads_ref, gain_ref):
    total = jnp.sum(sums_ref[:, 0, : 2 * TOK], axis=0, keepdims=True)
    for row, at in enumerate((0, SIZE, TOK)):
        for g in range(GROUPS):
            piece = total[:, at + 16 * g : at + 16 * g + GH]
            heads_ref[row : row + 1, GH * g : GH * (g + 1)] = piece
    gains = sums_ref[:, 0, 2 * TOK :]
    parts = gains.shape[0] // blocks
    gains = sum(gains[blocks * d : blocks * (d + 1)] for d in range(parts))
    for i in range(WIDTH // TOK):
        gain_ref[:, TOK * i : TOK * (i + 1)] = gains[i : i + 1]


def shape(dims, dtype):
    return jax.ShapeDtypeStruct(dims, dtype)


MIB = 1024 * 1024
VMEM = pl.BlockSpec(memory_space=pltpu.VMEM)
SMEM = pl.BlockSpec(memory_space=pltpu.SMEM)


def call(kernel, outs, args, scratch=(), tables=(), mib=32, us=5):
    single = not isinstance(outs, tuple)
    return pl.pallas_call(
        kernel,
        out_shape=outs,
        in_specs=[SMEM if i in tables else VMEM for i in range(len(args))],
        out_specs=VMEM if single else (VMEM,) * len(outs),
        scratch_shapes=list(scratch),
        compiler_params=pltpu.CompilerParams(vmem_limit_bytes=mib * MIB),
        cost_estimate=pl.CostEstimate(flops=int(us * 1e9), bytes_accessed=8 * MIB, transcendentals=0),
    )(*args)


def local(
    mamba_in,
    step_raw,
    state_in,
    state_out,
    log_rate,
    step_bias,
    skip_gain,
    norm_gain,
    doc_lengths,
    doc_moved,
    queries,
    attn_keys,
    attn_grad,
):
    x, raw, q, k = mamba_in[0], step_raw[0], queries[0], attn_keys[0]
    in_map, map_in = jnp.transpose(state_in[0]), jnp.transpose(state_out[0])
    lengths, moved = jnp.transpose(doc_lengths[0]), jnp.transpose(doc_moved[0])
    rate, bias, skip = log_rate[None], step_bias[None], skip_gain[None]
    blocks = lax.axis_size("ctx")
    devices = blocks * lax.axis_size("dp")
    rows = 8 * blocks
    swap = [(i, i ^ (blocks // 2)) for i in range(blocks)]
    wide = (TOK, WIDTH)
    decay_scratch = [pltpu.VMEM((GROUPS, TOK, TOK), F32), pltpu.VMEM((SIZE, TOK), F32)]
    probs_shape = (GROUPS * AH, TOK, TOK)

    def exchange(value):
        value = value.reshape(blocks, 8, value.shape[1])
        value = lax.all_to_all(value, "ctx", 0, 0, tiled=True)
        return value.reshape(rows, value.shape[2])

    back = lax.ppermute(attn_grad[0, TOK:], "ctx", swap)
    message = call(
        states_kernel, shape((rows, GW + 128), BF16), (x, raw, in_map, rate, bias), mib=8
    )
    gathered = exchange(message)
    wide_scratch = [pltpu.VMEM((rows, GW), F32)]
    firsts = call(
        functools.partial(scan_kernel, blocks, False),
        shape((rows, GW), BF16),
        (gathered,),
        wide_scratch,
        mib=8,
        us=2,
    )
    start = exchange(firsts)
    inner, probs = call(
        inner_kernel,
        (shape(wide, F32), shape(probs_shape, F32)),
        (x, raw, in_map, map_in, rate, bias, skip, lengths, moved, q, k),
        decay_scratch,
        tables=(7, 8),
        us=8,
    )
    gv, home = call(
        value_grad_kernel,
        (shape(wide, BF16), shape(wide, BF16)),
        (lengths, moved, probs, attn_grad[0], back),
        tables=(0, 1),
        us=5,
    )
    y, values, low, message = call(
        norm_kernel,
        (shape(wide, F32), shape(wide, BF16), shape(wide, BF16), shape((rows, GW + 128), BF16)),
        (raw, map_in, rate, bias, norm_gain[None], start, inner, gv),
        [pltpu.VMEM(wide, F32), pltpu.VMEM((32, TOK), F32)],
        us=7,
    )
    attn, packed, gq, gk = call(
        attention_kernel,
        (shape((TOK + SEND, WIDTH), BF16), shape((SEND, WIDTH), BF16), shape(wide, BF16), shape(wide, BF16)),
        (lengths, moved, q, k, values, probs, home),
        tables=(0, 1),
        us=8,
    )
    arrived = lax.ppermute(packed, "ctx", swap)
    lasts, gain_sum = call(
        functools.partial(scan_kernel, blocks, True),
        (shape((rows, GW), BF16), shape((1, TOK), F32)),
        (exchange(message), gathered),
        wide_scratch,
        mib=8,
        us=2,
    )
    state_grad = exchange(lasts)
    dx, flow, direct, gout, gin, skip_sum = call(
        inner_back_kernel,
        (
            shape(wide, F32),
            shape((TOK, TOK), F32),
            shape((TOK, TOK), F32),
            shape((SIZE, TOK), BF16),
            shape((SIZE, TOK), F32),
            shape((1, TOK), F32),
        ),
        (x, raw, in_map, map_in, rate, bias, skip, start, y, low),
        decay_scratch + [pltpu.VMEM((SIZE, TOK), F32)],
        us=8,
    )
    gx, gin, gstep, sums = call(
        late_kernel,
        (
            shape(wide, BF16),
            shape((SIZE, TOK), BF16),
            shape((HEADS, TOK), F32),
            shape((devices, 1, 3 * TOK), F32),
        ),
        (x, raw, in_map, rate, bias, start, state_grad, dx, flow, direct, gin, skip_sum, gain_sum),
        us=6,
    )
    sums = lax.all_to_all(sums, ("dp", "ctx"), 0, 0, tiled=True)
    attn = lax.dynamic_update_slice(attn, arrived, (TOK, 0))
    heads, gain = call(
        functools.partial(last_kernel, blocks),
        (shape((3, HEADS), F32), shape((1, WIDTH), F32)),
        (sums,),
        mib=4,
        us=1,
    )
    return (
        attn[None],
        gq[None],
        gk[None],
        gx[None],
        jnp.transpose(gin)[None],
        jnp.transpose(gout)[None],
        gstep[None],
        heads,
        gain[0],
    )


def solution(mesh):
    in_specs = (
        P("dp", "ctx", None),
        P("dp", None, "ctx"),
        P("dp", "ctx", None),
        P("dp", "ctx", None),
        P(),
        P(),
        P(),
        P(),
        P("dp", None, None),
        P("dp", None, None),
        P("dp", "ctx", None),
        P("dp", "ctx", None),
        P("dp", "ctx", None),
    )
    out_specs = (
        P("dp", "ctx", None),
        P("dp", "ctx", None),
        P("dp", "ctx", None),
        P("dp", "ctx", None),
        P("dp", "ctx", None),
        P("dp", "ctx", None),
        P("dp", None, "ctx"),
        P(),
        P(),
    )
    return jax.shard_map(local, mesh=mesh, in_specs=in_specs, out_specs=out_specs, check_vma=False)
```

```python
import functools
import math

import jax
import jax.numpy as jnp
from jax import lax
from jax.experimental import pallas as pl
from jax.experimental.pallas import tpu as pltpu
from jax.sharding import PartitionSpec as P

F32 = jnp.float32
BF16 = jnp.bfloat16
HIGH = lax.Precision.HIGHEST
EPSILON = 1e-05
MASKED = -1e30

TOK = 128
HEADS = 56
SIZE = 64
GROUPS = 4
GW = 896
GH = 14
AH = 4
ASIZE = 224
WIDTH = GROUPS * GW
SEND = 64
WINDOWS = ((0, 2), (1, 3), (3, 3), (5, 2))

NT = (((1,), (1,)), ((), ()))
TN = (((0,), (0,)), ((), ()))


def dot(a, b, dims=(((1,), (0,)), ((), ())), precision=None):
    return lax.dot_general(a, b, dims, precision=precision, preferred_element_type=F32)


def iota(shape, dim):
    return lax.broadcasted_iota(jnp.int32, shape, dim)


def pad_heads(rows):
    gap = jnp.zeros((2, rows.shape[1]), rows.dtype)
    parts = []
    for g in range(GROUPS):
        parts += [rows[g * GH : (g + 1) * GH], gap]
    return jnp.concatenate(parts, axis=0)


def unpad_heads(rows):
    return jnp.concatenate([rows[16 * g : 16 * g + GH] for g in range(GROUPS)], axis=0)


def columns(*rows):
    stack = jnp.concatenate(list(rows) + [jnp.zeros((8 - len(rows), HEADS), F32)], axis=0)
    stack = jnp.concatenate([stack, jnp.zeros((8, 128 - HEADS), F32)], axis=1)
    turned = pad_heads(jnp.transpose(stack)[:HEADS])
    return [turned[:, i : i + 1] for i in range(len(rows))]


def expander(group, parts=2):
    shape = (64 * parts, GW)
    return jnp.where(
        (iota(shape, 0) & 63) == (iota(shape, 1) >> 6) + 16 * group, 1.0, 0.0
    ).astype(BF16)


def split(value):
    high = value.astype(BF16)
    low = (value - high.astype(F32)).astype(BF16)
    return high, low


def stacked_parts(value):
    high, low = split(value)
    return jnp.transpose(jnp.concatenate([high.astype(F32), low.astype(F32)], axis=0)).astype(BF16)


def decay_sums(raw, bias, rate):
    z = pad_heads(raw) + bias
    step = jnp.maximum(z, 0.0) + jnp.log1p(jnp.exp(-jnp.abs(z)))
    neg = -jnp.exp(rate)
    tri = jnp.where(iota((TOK, TOK), 0) <= iota((TOK, TOK), 1), 1.0, 0.0)
    running = dot(neg * step, tri, precision=HIGH)
    return z, step, neg, running


def chunk(g, size):
    return pl.ds(g * size if isinstance(g, int) else pl.multiple_of(g * size, size), size)


def lanes(g):
    return chunk(g, GW)


def rows64(g):
    return chunk(g, SIZE)


def by_lane(ref, g):
    return ref.at[:, lanes(g)]


def by_lane_top(ref, g):
    return ref.at[pl.ds(0, TOK), lanes(g)]


def by_row(ref, g):
    return ref.at[rows64(g), :]


def by_head(ref, g):
    return ref.at[pl.ds(AH * g, AH)]


def each_group(body, carry):
    for g in range(GROUPS):
        carry = body(g, carry)
    return carry


class Copies:
    def __init__(self, sem, *pairs):
        self.sem, self.pairs = sem, pairs

    def parts(self, g):
        made = []
        for i, (source, target, view, *other) in enumerate(self.pairs):
            view_to = other[0] if other else view
            made.append(
                pltpu.make_async_copy(view(source, g), view_to(target, g), self.sem.at[i, g])
            )
        return made

    def start(self, g):
        for copy in self.parts(g):
            copy.start()

    def wait(self, g):
        for copy in self.parts(g):
            copy.wait()

    def start_all(self, groups=range(GROUPS)):
        for g in groups:
            self.start(g)

    def wait_all(self, groups=range(GROUPS)):
        for g in groups:
            self.wait(g)


def states_kernel(
    x_hbm,
    raw_hbm,
    in_hbm,
    rate_hbm,
    bias_hbm,
    out_hbm,
    decays_ref,
    tail_ref,
    x_ref,
    raw_ref,
    in_ref,
    rate_ref,
    bias_ref,
    out_ref,
    sem,
    small,
    out_sem,
):
    smalls = [
        pltpu.make_async_copy(source, target, small.at[i])
        for i, (source, target) in enumerate(
            ((raw_hbm, raw_ref), (rate_hbm, rate_ref), (bias_hbm, bias_ref), (in_hbm, in_ref))
        )
    ]
    for copy in smalls:
        copy.start()
    fetch = Copies(sem, (x_hbm, x_ref, by_lane))
    fetch.start_all()
    put = Copies(out_sem, (out_ref, out_hbm, by_row))
    for copy in smalls:
        copy.wait()
    rate, bias = columns(rate_ref[...], bias_ref[...])
    z, step, neg, running = decay_sums(raw_ref[...], bias, rate)
    last = running[:, TOK - 1 :]
    tail = stacked_parts(jnp.exp(last - running) * step)
    total = stacked_parts(jnp.broadcast_to(jnp.exp(last), running.shape))[:SIZE]
    in_map = in_ref[...]
    for g in range(GROUPS):
        wide = dot(tail, expander(g))
        fetch.wait(g)
        scaled = (x_ref[:, g * GW : (g + 1) * GW].astype(F32) * wide).astype(BF16)
        out_ref[g * SIZE : (g + 1) * SIZE, :GW] = dot(in_map, scaled).astype(BF16)
        out_ref[g * SIZE : (g + 1) * SIZE, GW:] = total
        put.start(g)
    tail_ref[...] = tail
    for i, value in enumerate((z, step, jnp.broadcast_to(neg, z.shape), running)):
        decays_ref[i] = value
    put.wait_all()


def scan_kernel(blocks, reverse, *refs):
    if reverse:
        carry_ref, total_ref, out_ref, sum_ref, wide_ref = refs
        ones = jnp.ones((16, 8 * blocks), BF16)
        sum_ref[...] = dot(ones, carry_ref[:, GW:])[:1]
    else:
        carry_ref, out_ref, wide_ref = refs
        total_ref = carry_ref
    group = lax.axis_index("ctx") // 8
    wide_ref[...] = dot(total_ref[:, GW:], expander(group))
    state = jnp.zeros((8, GW), F32)
    pairs = range(blocks // 2)
    for i in reversed(pairs) if reverse else pairs:
        rows = slice(16 * i, 16 * i + 16)
        carry = carry_ref[rows, :GW].astype(F32)
        first = state
        at = slice(8, 16) if reverse else slice(0, 8)
        second = wide_ref[rows][at] * first + carry[at]
        at = slice(0, 8) if reverse else slice(8, 16)
        state = wide_ref[rows][at] * second + carry[at]
        both = [second, first] if reverse else [first, second]
        out_ref[rows, :] = jnp.concatenate(both, axis=0).astype(BF16)


def lane_masks():
    masks = []
    for i, (tile, tiles) in enumerate(WINDOWS):
        at = iota((1, 128 * tiles), 1) + 128 * tile
        masks.append(jnp.where((at >= ASIZE * i) & (at < ASIZE * (i + 1)), 1.0, 0.0).astype(BF16))
    return masks


def join_windows(parts):
    tiles = [None] * 7
    for (tile, count), part in zip(WINDOWS, parts):
        for k in range(count):
            piece = part[:, 128 * k : 128 * (k + 1)]
            tiles[tile + k] = piece if tiles[tile + k] is None else tiles[tile + k] + piece
    return jnp.concatenate(tiles, axis=1)


def pair_rows(tile):
    half = jnp.where(iota((1, 128), 1) < SIZE, 1.0, 0.0).astype(BF16)
    return jnp.concatenate([tile * half, tile * (1 - half)], axis=0)


def documents(lengths_ref, moved_ref):
    block = lax.axis_index("ctx")
    begin, sent, docs = jnp.int32(0), jnp.int32(0), []
    for d in range(8):
        length, moved = lengths_ref[d, block], moved_ref[d, block]
        end = begin + length
        limit = jnp.where(moved == 1, end, begin)
        docs.append((begin, end, limit, sent))
        sent = sent + (limit - begin)
        begin = end
    return docs


def place_slots(docs, dims, dim):
    at = iota(dims, dim)
    slots = jnp.full(dims, -1, jnp.int32)
    for begin, _, limit, sent in docs:
        slots = jnp.where((at >= begin) & (at < limit), at + (sent - begin), slots)
    return slots


def columns_of(running):
    turned = jnp.transpose(jnp.concatenate([running, running], axis=0))
    return [turned] + [pltpu.roll(turned, TOK - 16 * g, 1) for g in range(1, GROUPS)]


def local_decay(column, heads, h):
    return jnp.exp(jnp.minimum(column[:, h : h + 1] - heads[h : h + 1], 20.0))


def inner_kernel(
    x_hbm,
    decays_ref,
    in_ref,
    map_ref,
    skip_ref,
    y_hbm,
    grown_ref,
    skips_ref,
    x_ref,
    y_ref,
    column_ref,
    row_ref,
    sem,
    out_sem,
):
    fetch = Copies(sem, (x_hbm, x_ref, by_lane))
    put = Copies(out_sem, (y_ref, y_hbm, by_lane))
    fetch.start_all()
    square = (TOK, TOK)
    (skip,) = columns(skip_ref[...])
    step, running = decays_ref[1], decays_ref[3]
    skips = stacked_parts(jnp.broadcast_to(skip, (SIZE, TOK)))[:16]
    skips_ref[...] = skips
    grown_ref[...] = stacked_parts(jnp.exp(running))
    row_ref[...] = running - jnp.log(step)
    for g, column in enumerate(columns_of(running)):
        column_ref[g] = column
    causal = iota(square, 0) >= iota(square, 1)
    gram = jnp.where(causal, dot(map_ref[...], in_ref[...], TN), 0.0)

    def group(g, carry):
        at = lanes(g)
        fetch.wait(g)
        x = x_ref[:, at]
        heads = row_ref[chunk(g, 16), :]
        column = column_ref[g]
        inner = []
        for i in range(GH // 2):
            pair = [(local_decay(column, heads, h) * gram).astype(BF16) for h in (2 * i, 2 * i + 1)]
            rows = pair_rows(x[:, 128 * i : 128 * (i + 1)])
            inner.append(dot(jnp.concatenate(pair, axis=1), rows))
        y_ref[:, at] = jnp.concatenate(inner, axis=1) + dot(skips, expander(g))[:1] * x.astype(F32)
        put.start(g)
        return carry

    each_group(group, 0)
    put.wait_all()


def weights_kernel(
    lengths_ref,
    moved_ref,
    q_hbm,
    k_hbm,
    grad_hbm,
    probs_hbm,
    moved_hbm,
    q_ref,
    k_ref,
    rows_ref,
    probs_ref,
    sem,
    out_sem,
    moved_sem,
):
    fetch = Copies(sem, (q_hbm, q_ref, by_lane), (k_hbm, k_ref, by_lane))
    put = Copies(out_sem, (probs_ref, probs_hbm, by_head))
    arrive = pltpu.make_async_copy(grad_hbm.at[pl.ds(TOK, SEND), :], rows_ref, moved_sem.at[0])
    leave = pltpu.make_async_copy(rows_ref, moved_hbm, moved_sem.at[1])
    arrive.start()
    fetch.start_all()
    scale = 1.0 / math.sqrt(ASIZE)
    square = (TOK, TOK)
    at_q, at_k = iota(square, 0), iota(square, 1)
    docs = documents(lengths_ref, moved_ref)
    seg_q = jnp.zeros(square, jnp.int32)
    seg_k = jnp.zeros(square, jnp.int32)
    for _, end, _, _ in docs:
        seg_q += jnp.where(at_q >= end, 1, 0)
        seg_k += jnp.where(at_k >= end, 1, 0)
    allowed = (seg_q == seg_k) & (at_k <= at_q)
    masks = lane_masks()
    arrive.wait()
    leave.start()

    def group(g, carry):
        at = lanes(g)
        fetch.wait(g)
        q, k = q_ref[:, at], k_ref[:, at]
        for i, (tile, count) in enumerate(WINDOWS):
            window = slice(128 * tile, 128 * (tile + count))
            scores = dot(q[:, window] * masks[i], k[:, window], NT) * scale
            scores = jnp.where(allowed, scores, MASKED)
            weights = jnp.exp(scores - jnp.max(scores, axis=-1, keepdims=True))
            total = jnp.sum(weights, axis=-1, keepdims=True)
            probs_ref[AH * g + i] = weights * (1.0 / total)
        put.start(g)
        return carry

    each_group(group, 0)
    leave.wait()
    put.wait_all()


def value_grad_kernel(
    lengths_ref,
    moved_ref,
    probs_hbm,
    grad_hbm,
    back_hbm,
    gv_hbm,
    home_hbm,
    probs_ref,
    grad_ref,
    back_ref,
    gv_ref,
    home_ref,
    sem,
    out_sem,
):
    fetch = Copies(
        sem,
        (back_hbm, back_ref, by_lane),
        (grad_hbm, grad_ref, by_lane_top, by_lane),
        (probs_hbm, probs_ref, by_head),
    )
    put = Copies(out_sem, (gv_ref, gv_hbm, by_lane), (home_ref, home_hbm, by_lane))
    fetch.start_all()
    square = (TOK, TOK)
    docs = documents(lengths_ref, moved_ref)
    slots = place_slots(docs, square, 0)
    place = jnp.where(slots == iota(square, 1), 1.0, 0.0).astype(BF16)[:, :SEND]
    kept = jnp.where(slots < 0, 1.0, 0.0).astype(BF16)[:, :1]
    masks = lane_masks()

    def group(g, carry):
        at = lanes(g)
        fetch.wait(g)
        grad = grad_ref[:, at] * kept + dot(place, back_ref[:, at]).astype(BF16)
        home_ref[:, at] = grad
        parts = []
        for i, (tile, count) in enumerate(WINDOWS):
            window = slice(128 * tile, 128 * (tile + count))
            parts.append(dot(probs_ref[AH * g + i].astype(BF16), grad[:, window] * masks[i], TN))
        gv_ref[:, at] = join_windows(parts).astype(BF16)
        put.start(g)
        return carry

    each_group(group, 0)
    put.wait_all()


def norm_kernel(
    grown_ref,
    map_ref,
    gain_ref,
    start_ref,
    inner_hbm,
    gv_hbm,
    y_hbm,
    values_hbm,
    low_hbm,
    message_hbm,
    inner_ref,
    gv_ref,
    y_ref,
    values_ref,
    low_ref,
    message_ref,
    wide_ref,
    sums_ref,
    sem,
    y_sem,
    out_sem,
):
    fetch = Copies(sem, (inner_hbm, inner_ref, by_lane), (gv_hbm, gv_ref, by_lane))
    put_y = Copies(y_sem, (y_ref, y_hbm, by_lane))
    put = Copies(out_sem, (values_ref, values_hbm, by_lane), (low_ref, low_hbm, by_lane))
    fetch.start_all()
    grown = grown_ref[...]
    map_in = map_ref[...]
    out_rows = jnp.transpose(map_in.astype(F32)).astype(BF16)
    power = jnp.zeros((TOK, 1), F32)
    along = jnp.zeros((TOK, 1), F32)
    for g in range(GROUPS):
        at = slice(g * GW, (g + 1) * GW)
        wide = dot(grown, expander(g))
        wide_ref[:, at] = wide
        carried = dot(out_rows, start_ref[g * SIZE : (g + 1) * SIZE, :]) * wide
        fetch.wait(g)
        y = inner_ref[:, at] + carried
        y_ref[:, at] = y
        put_y.start(g)
        power = power + jnp.sum(y * y, axis=-1, keepdims=True)
        scaled = gv_ref[:, at].astype(F32) * gain_ref[:, at]
        along = along + jnp.sum(scaled * y, axis=-1, keepdims=True)
    inverse = lax.rsqrt(power * (1.0 / WIDTH) + EPSILON)
    slope = inverse * inverse * inverse * along * (1.0 / WIDTH)
    sums_ref[...] = jnp.zeros_like(sums_ref)
    for g in range(GROUPS):
        at = slice(g * GW, (g + 1) * GW)
        rows = slice(g * SIZE, (g + 1) * SIZE)
        y, gain, gv = y_ref[:, at], gain_ref[:, at], gv_ref[:, at].astype(F32)
        normed = y * inverse
        values_ref[:, at] = (normed * gain).astype(BF16)
        gain_sum = jnp.sum(gv * normed, axis=0, keepdims=True)
        for i in range(7):
            sums_ref[7 * g + i : 7 * g + i + 1, :] = gain_sum[:, 128 * i : 128 * (i + 1)]
        mixed_grad = gv * gain * inverse - y * slope
        low_ref[:, at] = mixed_grad.astype(BF16)
        put.start(g)
        grown_grad = (wide_ref[:, at] * mixed_grad).astype(BF16)
        message_ref[rows, :GW] = dot(map_in, grown_grad).astype(BF16)
    sums = sums_ref[...]
    high, low = split(sums)
    lowest = (sums - high.astype(F32) - low.astype(F32)).astype(BF16)
    dims = (message_ref.shape[0], 96)
    at, source = iota(dims, 0), iota(dims, 1)
    spread = jnp.where((at >> 3 == source & 31) & (at & 7 == source >> 5), 1.0, 0.0).astype(BF16)
    message_ref[:, GW:] = dot(spread, jnp.concatenate([high, low, lowest], axis=0)).astype(BF16)
    last = pltpu.make_async_copy(message_ref, message_hbm, out_sem.at[2, 0])
    last.start()
    put_y.wait_all()
    put.wait_all()
    last.wait()


def attention_kernel(
    lengths_ref,
    moved_ref,
    values_hbm,
    probs_hbm,
    home_hbm,
    attn_hbm,
    packed_hbm,
    dscores_hbm,
    values_ref,
    probs_ref,
    home_ref,
    attn_ref,
    packed_ref,
    dscores_ref,
    sem,
    out_sem,
):
    fetch = Copies(
        sem,
        (probs_hbm, probs_ref, by_head),
        (values_hbm, values_ref, by_lane),
        (home_hbm, home_ref, by_lane),
    )
    put = Copies(
        out_sem,
        (packed_ref, packed_hbm, by_lane),
        (attn_ref, attn_hbm, by_lane, by_lane_top),
        (dscores_ref, dscores_hbm, by_head),
    )
    scale = 1.0 / math.sqrt(ASIZE)
    fetch.start_all()
    docs = documents(lengths_ref, moved_ref)
    pick = place_slots(docs, (SEND, TOK), 1) == iota((SEND, TOK), 0)
    pick = jnp.where(pick, 1.0, 0.0).astype(BF16)
    kept = jnp.where(place_slots(docs, (TOK, TOK), 0) < 0, 1.0, 0.0).astype(BF16)[:, :1]
    masks = lane_masks()

    def group(g, carry):
        at = lanes(g)
        fetch.wait(g)
        values, grad = values_ref[:, at], home_ref[:, at]
        outs = []
        for i, (tile, count) in enumerate(WINDOWS):
            window = slice(128 * tile, 128 * (tile + count))
            probs = probs_ref[AH * g + i]
            vals = values[:, window] * masks[i]
            outs.append(dot(probs.astype(BF16), vals))
            dprobs = dot(grad[:, window], vals, NT)
            delta = jnp.sum(probs * dprobs, axis=-1, keepdims=True)
            dscores_ref[AH * g + i] = (probs * (dprobs - delta) * scale).astype(BF16)
        head_out = join_windows(outs).astype(BF16)
        attn_ref[:, at] = head_out * kept
        packed_ref[:, at] = dot(pick, head_out).astype(BF16)
        put.start(g)
        return carry

    each_group(group, 0)
    put.wait_all()


def attention_grad_kernel(
    q_hbm,
    k_hbm,
    dscores_hbm,
    arrived_hbm,
    attn_in_hbm,
    gq_hbm,
    gk_hbm,
    attn_hbm,
    q_ref,
    k_ref,
    dscores_ref,
    gq_ref,
    gk_ref,
    rows_ref,
    sem,
    out_sem,
    arrived_sem,
):
    del attn_in_hbm
    fetch = Copies(
        sem,
        (dscores_hbm, dscores_ref, by_head),
        (k_hbm, k_ref, by_lane),
        (q_hbm, q_ref, by_lane),
    )
    put = Copies(out_sem, (gq_ref, gq_hbm, by_lane), (gk_ref, gk_hbm, by_lane))
    fetch.start_all()
    arrive = pltpu.make_async_copy(arrived_hbm, rows_ref, arrived_sem.at[0])
    leave = pltpu.make_async_copy(rows_ref, attn_hbm.at[pl.ds(TOK, SEND), :], arrived_sem.at[1])
    arrive.start()
    masks = lane_masks()

    arrive.wait()
    leave.start()

    def group(g, carry):
        at = lanes(g)
        fetch.wait(g)
        q, k = q_ref[:, at], k_ref[:, at]
        gqs, gks = [], []
        for i, (tile, count) in enumerate(WINDOWS):
            window = slice(128 * tile, 128 * (tile + count))
            dscores = dscores_ref[AH * g + i]
            gqs.append(dot(dscores, k[:, window] * masks[i]))
            gks.append(dot(dscores, q[:, window] * masks[i], TN))
        gq_ref[:, at] = join_windows(gqs).astype(BF16)
        gk_ref[:, at] = join_windows(gks).astype(BF16)
        put.start(g)
        return carry

    each_group(group, 0)
    leave.wait()
    put.wait_all()


def inner_back_kernel(
    x_hbm,
    decays_ref,
    in_ref,
    map_ref,
    skips_ref,
    grown_ref,
    start_hbm,
    y_hbm,
    low_hbm,
    dx_hbm,
    flow_ref,
    direct_ref,
    gout_ref,
    gin_ref,
    skip_sum_ref,
    x_ref,
    start_ref,
    y_ref,
    low_ref,
    dx_ref,
    column_ref,
    row_ref,
    sem,
    out_sem,
):
    fetch = Copies(
        sem,
        (low_hbm, low_ref, by_lane),
        (x_hbm, x_ref, by_lane),
        (start_hbm, start_ref, by_row),
        (y_hbm, y_ref, by_lane),
    )
    put = Copies(out_sem, (dx_ref, dx_hbm, by_lane))
    fetch.start_all()
    square = (TOK, TOK)
    causal = iota(square, 0) >= iota(square, 1)
    step, running = decays_ref[1], decays_ref[3]
    skips, grown = skips_ref[...], grown_ref[...]
    row_ref[...] = running - jnp.log(step)
    for g, column in enumerate(columns_of(running)):
        column_ref[g] = column
    in_map, map_in = in_ref[...], map_ref[...]
    gram = jnp.where(causal, dot(map_in, in_map, TN), 0.0)
    flow_ref[...] = jnp.zeros_like(flow_ref)
    direct_ref[...] = jnp.zeros_like(direct_ref)
    gout_ref[...] = jnp.zeros_like(gout_ref)

    def group(g, carry):
        gram_grad, skip_sum = carry
        at = lanes(g)
        fetch.wait(g)
        x, low_grad = x_ref[:, at], low_ref[:, at]
        mixed_grad = low_grad.astype(F32)
        wide = expander(g)
        grown_grad = (dot(grown, wide) * mixed_grad).astype(BF16)
        gout_ref[...] += dot(start_ref[rows64(g), :], grown_grad, NT)
        heads = row_ref[chunk(g, 16), :]
        column = column_ref[g]
        inner = []
        for i in range(GH // 2):
            tile = slice(128 * i, 128 * (i + 1))
            both = dot(low_grad[:, tile], pair_rows(x[:, tile]), NT)
            pair = []
            for j in (0, 1):
                decay = local_decay(column, heads, 2 * i + j)
                gram_grad = gram_grad + both[:, TOK * j : TOK * (j + 1)] * decay
                pair.append((decay * gram).astype(BF16))
            inner.append(dot(jnp.concatenate(pair, axis=0), pair_rows(low_grad[:, tile]), TN))
        inner = jnp.concatenate(inner, axis=1)
        wide_skip = dot(skips, wide)[:1]
        x = x.astype(F32)
        dx_ref[:, at] = inner + wide_skip * mixed_grad
        put.start(g)
        product = x * inner
        high, low = split(mixed_grad * (y_ref[:, at] - wide_skip * x) - product)
        flow_ref[...] += dot(high, wide, NT) + dot(low, wide, NT)
        high, low = split(product)
        direct_ref[...] += dot(high, wide, NT) + dot(low, wide, NT)
        high, low = split(jnp.broadcast_to(jnp.sum(mixed_grad * x, axis=0, keepdims=True), (16, GW)))
        skip_sum = skip_sum + dot(high, wide, NT) + dot(low, wide, NT)
        return gram_grad, skip_sum

    gram_grad, skip_sum = each_group(group, (jnp.zeros(square, F32), jnp.zeros((16, TOK), F32)))
    skip_sum_ref[...] = skip_sum[:1]
    gram_grad = jnp.where(causal, gram_grad, 0.0).astype(BF16)
    gout_ref[...] += dot(in_map, gram_grad, NT)
    gin_ref[...] = dot(map_in, gram_grad)
    put.wait_all()


def late_kernel(
    x_hbm,
    decays_ref,
    tail_ref,
    in_ref,
    start_hbm,
    grad_ref,
    dx_hbm,
    flow_ref,
    direct_ref,
    gout_ref,
    gin_ref,
    skip_ref,
    gain_sum_ref,
    gx_hbm,
    gin_out_ref,
    gout_out_ref,
    step_ref,
    sums_ref,
    x_ref,
    start_ref,
    dx_ref,
    gx_ref,
    sem,
    out_sem,
):
    fetch = Copies(
        sem,
        (x_hbm, x_ref, by_lane),
        (start_hbm, start_ref, by_row),
        (dx_hbm, dx_ref, by_lane),
    )
    put = Copies(out_sem, (gx_ref, gx_hbm, by_lane))
    fetch.start_all()
    z, step, neg, running = (decays_ref[i] for i in range(4))
    last = running[:, TOK - 1 :]
    tail = tail_ref[...]
    in_rows = jnp.transpose(in_ref[...].astype(F32)).astype(BF16)
    tail_sum = jnp.zeros((TOK, TOK), F32)
    overlap = jnp.zeros((16, TOK), F32)
    gin = gin_ref[...]
    for g in range(GROUPS):
        at = slice(g * GW, (g + 1) * GW)
        rows = slice(g * SIZE, (g + 1) * SIZE)
        grad = grad_ref[rows, :]
        wide = expander(g)
        weight = dot(tail, wide)
        late = dot(in_rows, grad) * weight
        fetch.wait(g)
        x = x_ref[:, at].astype(F32)
        gx_ref[:, at] = (dx_ref[:, at] + late).astype(BF16)
        put.start(g)
        gin = gin + dot(grad, (x * weight).astype(BF16), NT)
        high, low = split(x * late)
        tail_sum = tail_sum + dot(high, wide, NT) + dot(low, wide, NT)
        both = jnp.sum(start_ref[rows, :].astype(F32) * grad.astype(F32), axis=0, keepdims=True)
        high, low = split(jnp.broadcast_to(both, (16, GW)))
        overlap = overlap + dot(high, wide, NT) + dot(low, wide, NT)
    gin_out_ref[...] = gin.astype(BF16)
    gout_out_ref[...] = gout_ref[...].astype(BF16)
    tail_sum = jnp.transpose(tail_sum)[:SIZE]
    flow = jnp.transpose(flow_ref[...])[:SIZE]
    direct = jnp.transpose(direct_ref[...])[:SIZE]
    overlap = jnp.transpose(jnp.broadcast_to(overlap[:1], (TOK, TOK)))[:SIZE]
    tri = jnp.where(iota((TOK, TOK), 0) >= iota((TOK, TOK), 1), 1.0, 0.0)
    ahead = dot(flow - tail_sum, tri, precision=HIGH)
    ahead = ahead + jnp.sum(tail_sum, axis=1, keepdims=True) + jnp.exp(last) * overlap
    step_grad = (direct + tail_sum) / step + neg * ahead
    raw_grad = step_grad * (1.0 / (1.0 + jnp.exp(-z)))
    step_ref[...] = unpad_heads(raw_grad)
    rate_grad = jnp.sum(neg * step * ahead, axis=1, keepdims=True)
    bias_grad = jnp.sum(raw_grad, axis=1, keepdims=True)
    both = jnp.concatenate([rate_grad, bias_grad], axis=0)
    devices = sums_ref.shape[0]
    skip_sum = skip_ref[...]
    sums_ref[:, 0, 0:TOK] = jnp.transpose(jnp.broadcast_to(both, (TOK, TOK)))[:devices]
    sums_ref[:, 0, TOK : 2 * TOK] = jnp.broadcast_to(skip_sum, (devices, TOK))
    sums_ref[:, 0, 2 * TOK :] = jnp.broadcast_to(gain_sum_ref[...], (devices, TOK))
    put.wait_all()


def last_kernel(blocks, sums_ref, heads_ref, gain_ref):
    total = jnp.sum(sums_ref[:, 0, : 2 * TOK], axis=0, keepdims=True)
    for row, at in enumerate((0, SIZE, TOK)):
        for g in range(GROUPS):
            piece = total[:, at + 16 * g : at + 16 * g + GH]
            heads_ref[row : row + 1, GH * g : GH * (g + 1)] = piece
    gains = sums_ref[:, 0, 2 * TOK :]
    parts = gains.shape[0] // blocks
    gains = sum(gains[blocks * d : blocks * (d + 1)] for d in range(parts))
    for i in range(WIDTH // TOK):
        gain_ref[pl.ds(TOK * i, TOK)] = gains[i]


MIB = 1024 * 1024
SMEM = pl.BlockSpec(memory_space=pltpu.SMEM)
VMEM = pl.BlockSpec(memory_space=pltpu.VMEM)


def call(kernel, args, outs, scratch=(), mib=32, us=5, aliases=None):
    specs = {
        "v": VMEM,
        "h": pl.BlockSpec(memory_space=pltpu.HBM),
        "a": VMEM,
        "s": SMEM,
    }
    kept = {"v": pltpu.VMEM, "h": pltpu.HBM}
    made = {"v": pltpu.VMEM, "h": pltpu.HBM, "a": jax.ShapeDtypeStruct}
    arrays = [
        pltpu.with_memory_space_constraint(array, kept[space]) if space in kept else array
        for space, array in args
    ]
    return pl.pallas_call(
        kernel,
        out_shape=tuple(made[space](dims, dtype) for space, dims, dtype in outs),
        in_specs=[specs[space] for space, _ in args],
        out_specs=tuple(specs[space] for space, _, _ in outs),
        scratch_shapes=list(scratch),
        input_output_aliases=aliases or {},
        compiler_params=pltpu.CompilerParams(vmem_limit_bytes=mib * MIB),
        cost_estimate=pl.CostEstimate(flops=int(us * 1e9), bytes_accessed=8 * MIB, transcendentals=0),
    )(*arrays)


def local(
    mamba_in,
    step_raw,
    state_in,
    state_out,
    log_rate,
    step_bias,
    skip_gain,
    norm_gain,
    doc_lengths,
    doc_moved,
    queries,
    attn_keys,
    attn_grad,
):
    x, raw, q, k, grad = mamba_in[0], step_raw[0], queries[0], attn_keys[0], attn_grad[0]
    in_map, map_in = jnp.transpose(state_in[0]), jnp.transpose(state_out[0])
    tables = [("s", jnp.transpose(doc_lengths[0])), ("s", jnp.transpose(doc_moved[0]))]
    rate, bias, skip = log_rate[None], step_bias[None], skip_gain[None]
    blocks = lax.axis_size("ctx")
    devices = blocks * lax.axis_size("dp")
    rows = 8 * blocks
    swap = [(i, i ^ (blocks // 2)) for i in range(blocks)]
    wide, square, sent = (TOK, WIDTH), (TOK, TOK), (SEND, WIDTH)
    maps, probs_shape = (SIZE, TOK), (GROUPS * AH, TOK, TOK)
    message_shape, states_shape = (rows, GW + 128), (rows, GW)
    decay_scratch = [pltpu.VMEM((GROUPS, TOK, TOK), F32), pltpu.VMEM(maps, F32)]

    def vmem(dims, dtype=BF16):
        return pltpu.VMEM(dims, dtype)

    def sems(*dims):
        return pltpu.SemaphoreType.DMA(dims)

    def exchange(value):
        value = value.reshape(blocks, 8, value.shape[1])
        value = lax.all_to_all(value, "ctx", 0, 0, tiled=True)
        return value.reshape(rows, value.shape[2])

    decays_shape = (4, SIZE, TOK)
    message, decays, tail = call(
        states_kernel,
        [("h", x), ("h", raw), ("h", in_map), ("h", rate), ("h", bias)],
        [("h", message_shape, BF16), ("a", decays_shape, F32), ("a", square, BF16)],
        [
            vmem(wide),
            vmem((HEADS, TOK), F32),
            vmem(maps),
            vmem((1, HEADS), F32),
            vmem((1, HEADS), F32),
            vmem(message_shape),
            sems(1, GROUPS),
            sems(4),
            sems(1, GROUPS),
        ],
        us=3,
    )
    gathered = exchange(message)
    probs, moving = call(
        weights_kernel,
        tables + [("h", q), ("h", k), ("h", grad)],
        [("h", probs_shape, F32), ("h", sent, BF16)],
        [
            vmem(wide),
            vmem(wide),
            vmem(sent),
            vmem(probs_shape, F32),
            sems(2, GROUPS),
            sems(1, GROUPS),
            sems(2),
        ],
        us=5,
    )
    back = lax.ppermute(moving, "ctx", swap)
    (firsts,) = call(
        functools.partial(scan_kernel, blocks, False),
        [("a", gathered)],
        [("a", states_shape, BF16)],
        [vmem(states_shape, F32)],
        mib=8,
        us=2,
    )
    start = exchange(firsts)
    decays, tail = ("a", decays), ("a", tail)
    inner, grown, skips = call(
        inner_kernel,
        [("h", x), decays, ("a", in_map), ("a", map_in), ("a", skip)],
        [("h", wide, F32), ("a", square, BF16), ("a", (16, TOK), BF16)],
        [vmem(wide), vmem(wide, F32)] + decay_scratch + [sems(1, GROUPS), sems(1, GROUPS)],
        us=5,
    )
    gv, home = call(
        value_grad_kernel,
        tables + [("h", probs), ("h", grad), ("h", back)],
        [("h", wide, BF16), ("h", wide, BF16)],
        [
            vmem(probs_shape, F32),
            vmem(wide),
            vmem(sent),
            vmem(wide),
            vmem(wide),
            sems(3, GROUPS),
            sems(2, GROUPS),
        ],
        us=4,
    )
    y, values, low, message = call(
        norm_kernel,
        [
            ("a", grown),
            ("a", map_in),
            ("a", norm_gain[None]),
            ("a", start),
            ("h", inner),
            ("h", gv),
        ],
        [("h", wide, F32), ("h", wide, BF16), ("h", wide, BF16), ("h", message_shape, BF16)],
        [
            vmem(wide, F32),
            vmem(wide),
            vmem(wide, F32),
            vmem(wide),
            vmem(wide),
            vmem(message_shape),
            vmem(wide, F32),
            vmem((32, TOK), F32),
            sems(2, GROUPS),
            sems(1, GROUPS),
            sems(3, GROUPS),
        ],
        us=4,
    )
    attn, packed, dscores = call(
        attention_kernel,
        tables + [("h", values), ("h", probs), ("h", home)],
        [("h", (TOK + SEND, WIDTH), BF16), ("h", sent, BF16), ("h", probs_shape, BF16)],
        [
            vmem(wide),
            vmem(probs_shape, F32),
            vmem(wide),
            vmem(wide),
            vmem(sent),
            vmem(probs_shape),
            sems(3, GROUPS),
            sems(3, GROUPS),
        ],
        us=5,
    )
    arrived = lax.ppermute(packed, "ctx", swap)
    received = exchange(message)
    lasts, gain_sum = call(
        functools.partial(scan_kernel, blocks, True),
        [("a", received), ("a", gathered)],
        [("a", states_shape, BF16), ("a", (1, TOK), F32)],
        [vmem(states_shape, F32)],
        mib=8,
        us=2,
    )
    state_grad = exchange(lasts)
    dx, *partial = call(
        inner_back_kernel,
        [("h", x), decays, ("a", in_map), ("a", map_in), ("a", skips), ("a", grown)]
        + [("h", start), ("h", y), ("h", low)],
        [
            ("h", wide, F32),
            ("a", square, F32),
            ("a", square, F32),
            ("a", maps, F32),
            ("a", maps, F32),
            ("a", (1, TOK), F32),
        ],
        [vmem(wide), vmem(states_shape), vmem(wide, F32), vmem(wide), vmem(wide, F32)]
        + decay_scratch
        + [sems(4, GROUPS), sems(1, GROUPS)],
        us=8,
    )
    gx, gin, gout, gstep, sums = call(
        late_kernel,
        [("h", x), decays, tail, ("a", in_map), ("h", start)]
        + [("a", state_grad), ("h", dx)]
        + [("a", part) for part in partial]
        + [("a", gain_sum)],
        [
            ("h", wide, BF16),
            ("a", maps, BF16),
            ("a", maps, BF16),
            ("a", (HEADS, TOK), F32),
            ("a", (devices, 1, 3 * TOK), F32),
        ],
        [vmem(wide), vmem(states_shape), vmem(wide, F32), vmem(wide), sems(3, GROUPS), sems(1, GROUPS)],
        us=5,
    )
    sums = lax.all_to_all(sums, ("dp", "ctx"), 0, 0, tiled=True)
    gq, gk, attn = call(
        attention_grad_kernel,
        [("h", q), ("h", k), ("h", dscores), ("h", arrived), ("h", attn)],
        [("h", wide, BF16), ("h", wide, BF16), ("h", (TOK + SEND, WIDTH), BF16)],
        [
            vmem(wide),
            vmem(wide),
            vmem(probs_shape),
            vmem(wide),
            vmem(wide),
            vmem(sent),
            sems(3, GROUPS),
            sems(2, GROUPS),
            sems(2),
        ],
        us=6,
        aliases={4: 2},
    )
    heads, gain = call(
        functools.partial(last_kernel, blocks),
        [("a", sums)],
        [("a", (3, HEADS), F32), ("a", (WIDTH,), F32)],
        mib=4,
        us=1,
    )
    return (
        attn[None],
        gq[None],
        gk[None],
        gx[None],
        jnp.transpose(gin)[None],
        jnp.transpose(gout)[None],
        gstep[None],
        heads,
        gain,
    )


def solution(mesh):
    in_specs = (
        P("dp", "ctx", None),
        P("dp", None, "ctx"),
        P("dp", "ctx", None),
        P("dp", "ctx", None),
        P(),
        P(),
        P(),
        P(),
        P("dp", None, None),
        P("dp", None, None),
        P("dp", "ctx", None),
        P("dp", "ctx", None),
        P("dp", "ctx", None),
    )
    out_specs = (
        P("dp", "ctx", None),
        P("dp", "ctx", None),
        P("dp", "ctx", None),
        P("dp", "ctx", None),
        P("dp", "ctx", None),
        P("dp", "ctx", None),
        P("dp", None, "ctx"),
        P(),
        P(),
    )
    return jax.shard_map(local, mesh=mesh, in_specs=in_specs, out_specs=out_specs, check_vma=False)
```

```python
import functools
import math

import jax
import jax.numpy as jnp
from jax import lax
from jax.experimental import pallas as pl
from jax.experimental.pallas import tpu as pltpu
from jax.sharding import PartitionSpec as P

F32 = jnp.float32
BF16 = jnp.bfloat16
EPSILON = 1e-05
MASKED = -1e30

TOK = 128
HEADS = 56
SIZE = 64
GROUPS = 4
GW = 896
GH = 14
AH = 4
ASIZE = 224
WIDTH = GROUPS * GW
SEND = 64
WINDOWS = ((0, 2), (1, 3), (3, 3), (5, 2))

NT = (((1,), (1,)), ((), ()))
TN = (((0,), (0,)), ((), ()))


def dot(a, b, dims=(((1,), (0,)), ((), ())), precision=None):
    return lax.dot_general(a, b, dims, precision=precision, preferred_element_type=F32)


def iota(shape, dim):
    return lax.broadcasted_iota(jnp.int32, shape, dim)


def pad_heads(rows):
    gap = jnp.zeros((2, rows.shape[1]), rows.dtype)
    parts = []
    for g in range(GROUPS):
        parts += [rows[g * GH : (g + 1) * GH], gap]
    return jnp.concatenate(parts, axis=0)


def unpad_heads(rows):
    return jnp.concatenate([rows[16 * g : 16 * g + GH] for g in range(GROUPS)], axis=0)


def columns(*rows):
    stack = jnp.concatenate(list(rows) + [jnp.zeros((8 - len(rows), HEADS), F32)], axis=0)
    stack = jnp.concatenate([stack, jnp.zeros((8, 128 - HEADS), F32)], axis=1)
    turned = pad_heads(jnp.transpose(stack)[:HEADS])
    return [turned[:, i : i + 1] for i in range(len(rows))]


def expander(group, parts=2):
    shape = (64 * parts, GW)
    return jnp.where(
        (iota(shape, 0) & 63) == (iota(shape, 1) >> 6) + 16 * group, 1.0, 0.0
    ).astype(BF16)


def split(value):
    high = value.astype(BF16)
    low = (value - high.astype(F32)).astype(BF16)
    return high, low


def stacked_parts(value):
    high, low = split(value)
    return jnp.transpose(jnp.concatenate([high.astype(F32), low.astype(F32)], axis=0)).astype(BF16)


def sums_by(value, chosen):
    high, low = split(value)
    lowest = (value - high.astype(F32) - low.astype(F32)).astype(BF16)
    ones = jnp.where(chosen, 1.0, 0.0).astype(BF16)
    return dot(jnp.concatenate([high, low, lowest], axis=1), jnp.concatenate([ones] * 3, axis=0))


def decay_sums(raw, bias, rate):
    z = pad_heads(raw) + bias
    step = jnp.maximum(z, 0.0) + jnp.log1p(jnp.exp(-jnp.abs(z)))
    neg = -jnp.exp(rate)
    running = sums_by(neg * step, iota((TOK, TOK), 0) <= iota((TOK, TOK), 1))
    return z, step, neg, running


def chunk(g, size, groups=1):
    return pl.ds(g * size, groups * size)


def lanes(g, groups=1):
    return chunk(g, GW, groups)


def rows64(g, groups=1):
    return chunk(g, SIZE, groups)


def by_lane(ref, g, groups):
    return ref.at[:, lanes(g, groups)]


def by_lane_top(ref, g, groups):
    return ref.at[pl.ds(0, TOK), lanes(g, groups)]


def by_row(ref, g, groups):
    return ref.at[rows64(g, groups), :]


def by_state_row(ref, g, groups):
    return ref.at[rows64(g, groups), pl.ds(0, GW)]


def by_head(ref, g, groups):
    return ref.at[chunk(g, AH, groups)]


def each_group(body, carry):
    for g in range(GROUPS):
        carry = body(g, carry)
    return carry


class Copies:
    def __init__(self, sem, *pairs, span=1):
        self.sem, self.pairs, self.span = sem, pairs, span

    def parts(self, g):
        made = []
        for i, (source, target, view, *other) in enumerate(self.pairs):
            view_to = other[0] if other else view
            source, target = view(source, g, self.span), view_to(target, g, self.span)
            made.append(pltpu.make_async_copy(source, target, self.sem.at[i, g]))
        return made

    def start(self, g):
        if (g + 1) % self.span == 0:
            for copy in self.parts(g + 1 - self.span):
                copy.start()

    def wait(self, g):
        if g % self.span == 0:
            for copy in self.parts(g):
                copy.wait()

    def start_all(self):
        for g in range(GROUPS):
            self.start(g)

    def wait_all(self):
        for g in range(GROUPS):
            self.wait(g)


def states_kernel(
    x_hbm,
    raw_hbm,
    in_hbm,
    rate_hbm,
    bias_hbm,
    out_hbm,
    decays_ref,
    tail_ref,
    x_ref,
    raw_ref,
    in_ref,
    rate_ref,
    bias_ref,
    out_ref,
    sem,
    small,
    out_sem,
):
    smalls = [
        pltpu.make_async_copy(source, target, small.at[i])
        for i, (source, target) in enumerate(
            ((raw_hbm, raw_ref), (rate_hbm, rate_ref), (bias_hbm, bias_ref), (in_hbm, in_ref))
        )
    ]
    for copy in smalls:
        copy.start()
    fetch = Copies(sem, (x_hbm, x_ref, by_lane), span=4)
    fetch.start_all()
    put = Copies(out_sem, (out_ref, out_hbm, by_row))
    for copy in smalls:
        copy.wait()
    rate, bias = columns(rate_ref[...], bias_ref[...])
    z, step, neg, running = decay_sums(raw_ref[...], bias, rate)
    last = running[:, TOK - 1 :]
    tail = stacked_parts(jnp.exp(last - running) * step)
    total = stacked_parts(jnp.broadcast_to(jnp.exp(last), running.shape))[:SIZE]
    in_map = in_ref[...]
    for g in range(GROUPS):
        wide = dot(tail, expander(g))
        fetch.wait(g)
        scaled = (x_ref[:, g * GW : (g + 1) * GW].astype(F32) * wide).astype(BF16)
        out_ref[g * SIZE : (g + 1) * SIZE, :GW] = dot(in_map, scaled).astype(BF16)
        out_ref[g * SIZE : (g + 1) * SIZE, GW:] = total
        put.start(g)
    tail_ref[...] = tail
    for i, value in enumerate((z, step, jnp.broadcast_to(neg, z.shape), running)):
        decays_ref[i] = value
    put.wait_all()


def scan_kernel(blocks, reverse, *refs):
    if reverse:
        carry_ref, total_ref, out_ref, sum_ref, wide_ref = refs
        ones = jnp.ones((16, 8 * blocks), BF16)
        sum_ref[...] = dot(ones, carry_ref[:, GW:])[:1]
    else:
        carry_ref, out_ref, total_ref, wide_ref = refs
        total_ref[...] = carry_ref[:, GW:]
    group = lax.axis_index("ctx") // 8
    wide_ref[...] = dot(total_ref[...], expander(group))
    state = jnp.zeros((8, GW), F32)
    pairs = range(blocks // 2)
    for i in reversed(pairs) if reverse else pairs:
        rows = slice(16 * i, 16 * i + 16)
        carry = carry_ref[rows, :GW].astype(F32)
        first = state
        at = slice(8, 16) if reverse else slice(0, 8)
        second = wide_ref[rows][at] * first + carry[at]
        at = slice(0, 8) if reverse else slice(8, 16)
        state = wide_ref[rows][at] * second + carry[at]
        both = [second, first] if reverse else [first, second]
        out_ref[rows, :] = jnp.concatenate(both, axis=0).astype(BF16)


def lane_masks():
    masks = []
    for i, (tile, tiles) in enumerate(WINDOWS):
        at = iota((1, 128 * tiles), 1) + 128 * tile
        masks.append(jnp.where((at >= ASIZE * i) & (at < ASIZE * (i + 1)), 1.0, 0.0).astype(BF16))
    return masks


def join_windows(parts):
    tiles = [None] * 7
    for (tile, count), part in zip(WINDOWS, parts):
        for k in range(count):
            piece = part[:, 128 * k : 128 * (k + 1)]
            tiles[tile + k] = piece if tiles[tile + k] is None else tiles[tile + k] + piece
    return jnp.concatenate(tiles, axis=1)


def pair_rows(tile):
    half = jnp.where(iota((1, 128), 1) < SIZE, 1.0, 0.0).astype(BF16)
    return jnp.concatenate([tile * half, tile * (1 - half)], axis=0)


def documents(lengths_ref, moved_ref):
    block = lax.axis_index("ctx")
    begin, sent, docs = jnp.int32(0), jnp.int32(0), []
    for d in range(8):
        length, moved = lengths_ref[d, block], moved_ref[d, block]
        end = begin + length
        limit = jnp.where(moved == 1, end, begin)
        docs.append((begin, end, limit, sent))
        sent = sent + (limit - begin)
        begin = end
    return docs


def place_slots(docs, dims, dim):
    at = iota(dims, dim)
    slots = jnp.full(dims, -1, jnp.int32)
    for begin, _, limit, sent in docs:
        slots = jnp.where((at >= begin) & (at < limit), at + (sent - begin), slots)
    return slots


def columns_of(running):
    turned = jnp.transpose(jnp.concatenate([running, running], axis=0))
    return [turned] + [pltpu.roll(turned, TOK - 16 * g, 1) for g in range(1, GROUPS)]


def local_decay(column, heads, h):
    return jnp.exp(jnp.minimum(column[:, h : h + 1] - heads[h : h + 1], 20.0))


def inner_kernel(
    x_hbm,
    decays_ref,
    in_ref,
    map_ref,
    skip_ref,
    y_ref,
    grown_ref,
    skips_ref,
    x_ref,
    column_ref,
    row_ref,
    sem,
):
    fetch = Copies(sem, (x_hbm, x_ref, by_lane), span=2)
    fetch.start_all()
    square = (TOK, TOK)
    (skip,) = columns(skip_ref[...])
    step, running = decays_ref[1], decays_ref[3]
    skips = stacked_parts(jnp.broadcast_to(skip, (SIZE, TOK)))[:16]
    skips_ref[...] = skips
    grown_ref[...] = stacked_parts(jnp.exp(running))
    row_ref[...] = running - jnp.log(step)
    for g, column in enumerate(columns_of(running)):
        column_ref[g] = column
    causal = iota(square, 0) >= iota(square, 1)
    gram = jnp.where(causal, dot(map_ref[...], in_ref[...], TN), 0.0)

    def group(g, carry):
        at = lanes(g)
        fetch.wait(g)
        x = x_ref[:, at]
        heads = row_ref[chunk(g, 16), :]
        column = column_ref[g]
        inner = []
        for i in range(GH // 2):
            pair = [(local_decay(column, heads, h) * gram).astype(BF16) for h in (2 * i, 2 * i + 1)]
            rows = pair_rows(x[:, 128 * i : 128 * (i + 1)])
            inner.append(dot(jnp.concatenate(pair, axis=1), rows))
        y_ref[:, at] = jnp.concatenate(inner, axis=1) + dot(skips, expander(g))[:1] * x.astype(F32)
        return carry

    each_group(group, 0)


def weights_kernel(
    lengths_ref,
    moved_ref,
    q_hbm,
    k_hbm,
    grad_hbm,
    probs_hbm,
    moved_hbm,
    q_ref,
    k_ref,
    rows_ref,
    probs_ref,
    sem,
    out_sem,
    moved_sem,
):
    fetch = Copies(sem, (q_hbm, q_ref, by_lane), (k_hbm, k_ref, by_lane), span=4)
    put = Copies(out_sem, (probs_ref, probs_hbm, by_head))
    arrive = pltpu.make_async_copy(grad_hbm.at[pl.ds(TOK, SEND), :], rows_ref, moved_sem.at[0])
    leave = pltpu.make_async_copy(rows_ref, moved_hbm, moved_sem.at[1])
    arrive.start()
    fetch.start_all()
    scale = 1.0 / math.sqrt(ASIZE)
    square = (TOK, TOK)
    at_q, at_k = iota(square, 0), iota(square, 1)
    docs = documents(lengths_ref, moved_ref)
    seg_q = jnp.zeros(square, jnp.int32)
    seg_k = jnp.zeros(square, jnp.int32)
    for _, end, _, _ in docs:
        seg_q += jnp.where(at_q >= end, 1, 0)
        seg_k += jnp.where(at_k >= end, 1, 0)
    allowed = (seg_q == seg_k) & (at_k <= at_q)
    masks = lane_masks()
    arrive.wait()
    leave.start()

    def group(g, carry):
        at = lanes(g)
        fetch.wait(g)
        q, k = q_ref[:, at], k_ref[:, at]
        for i, (tile, count) in enumerate(WINDOWS):
            window = slice(128 * tile, 128 * (tile + count))
            scores = dot(q[:, window] * masks[i], k[:, window], NT) * scale
            scores = jnp.where(allowed, scores, MASKED)
            weights = jnp.exp(scores - jnp.max(scores, axis=-1, keepdims=True))
            total = jnp.sum(weights, axis=-1, keepdims=True)
            probs_ref[AH * g + i] = weights * (1.0 / total)
        put.start(g)
        return carry

    each_group(group, 0)
    leave.wait()
    put.wait_all()


def value_grad_kernel(
    lengths_ref,
    moved_ref,
    probs_hbm,
    grad_hbm,
    back_ref,
    gv_hbm,
    home_hbm,
    probs_ref,
    grad_ref,
    gv_ref,
    home_ref,
    sem,
    out_sem,
):
    fetch = Copies(
        sem,
        (grad_hbm, grad_ref, by_lane_top, by_lane),
        (probs_hbm, probs_ref, by_head),
        span=4,
    )
    put = Copies(out_sem, (gv_ref, gv_hbm, by_lane), (home_ref, home_hbm, by_lane))
    fetch.start_all()
    square = (TOK, TOK)
    docs = documents(lengths_ref, moved_ref)
    slots = place_slots(docs, square, 0)
    place = jnp.where(slots == iota(square, 1), 1.0, 0.0).astype(BF16)[:, :SEND]
    kept = jnp.where(slots < 0, 1.0, 0.0).astype(BF16)[:, :1]
    masks = lane_masks()

    def group(g, carry):
        at = lanes(g)
        fetch.wait(g)
        grad = grad_ref[:, at] * kept + dot(place, back_ref[:, at]).astype(BF16)
        home_ref[:, at] = grad
        parts = []
        for i, (tile, count) in enumerate(WINDOWS):
            window = slice(128 * tile, 128 * (tile + count))
            parts.append(dot(probs_ref[AH * g + i].astype(BF16), grad[:, window] * masks[i], TN))
        gv_ref[:, at] = join_windows(parts).astype(BF16)
        put.start(g)
        return carry

    each_group(group, 0)
    put.wait_all()


def norm_kernel(
    grown_ref,
    map_ref,
    gain_ref,
    start_ref,
    inner_ref,
    gv_hbm,
    y_hbm,
    values_hbm,
    low_hbm,
    message_hbm,
    gv_ref,
    y_ref,
    values_ref,
    low_ref,
    message_ref,
    wide_ref,
    sums_ref,
    sem,
    y_sem,
    out_sem,
    message_sem,
):
    fetch = Copies(sem, (gv_hbm, gv_ref, by_lane), span=4)
    put_y = Copies(y_sem, (y_ref, y_hbm, by_lane))
    put_message = Copies(message_sem, (message_ref, message_hbm, by_state_row))
    put = Copies(out_sem, (values_ref, values_hbm, by_lane), (low_ref, low_hbm, by_lane))
    fetch.start_all()
    grown = grown_ref[...]
    map_in = map_ref[...]
    out_rows = jnp.transpose(map_in.astype(F32)).astype(BF16)
    power = jnp.zeros((TOK, 1), F32)
    along = jnp.zeros((TOK, 1), F32)
    for g in range(GROUPS):
        at = slice(g * GW, (g + 1) * GW)
        wide = dot(grown, expander(g))
        wide_ref[:, at] = wide
        carried = dot(out_rows, start_ref[g * SIZE : (g + 1) * SIZE, :]) * wide
        y = inner_ref[:, at] + carried
        y_ref[:, at] = y
        put_y.start(g)
        power = power + jnp.sum(y * y, axis=-1, keepdims=True)
    for g in range(GROUPS):
        at = slice(g * GW, (g + 1) * GW)
        fetch.wait(g)
        scaled = gv_ref[:, at].astype(F32) * gain_ref[:, at]
        along = along + jnp.sum(scaled * y_ref[:, at], axis=-1, keepdims=True)
    inverse = lax.rsqrt(power * (1.0 / WIDTH) + EPSILON)
    slope = inverse * inverse * inverse * along * (1.0 / WIDTH)
    sums_ref[...] = jnp.zeros_like(sums_ref)
    for g in range(GROUPS):
        at = slice(g * GW, (g + 1) * GW)
        rows = slice(g * SIZE, (g + 1) * SIZE)
        y, gain, gv = y_ref[:, at], gain_ref[:, at], gv_ref[:, at].astype(F32)
        normed = y * inverse
        values_ref[:, at] = (normed * gain).astype(BF16)
        gain_sum = jnp.sum(gv * normed, axis=0, keepdims=True)
        for i in range(7):
            sums_ref[7 * g + i : 7 * g + i + 1, :] = gain_sum[:, 128 * i : 128 * (i + 1)]
        mixed_grad = gv * gain * inverse - y * slope
        low_ref[:, at] = mixed_grad.astype(BF16)
        put.start(g)
        grown_grad = (wide_ref[:, at] * mixed_grad).astype(BF16)
        message_ref[rows, :GW] = dot(map_in, grown_grad).astype(BF16)
        put_message.start(g)
    sums = sums_ref[...]
    high, low = split(sums)
    lowest = (sums - high.astype(F32) - low.astype(F32)).astype(BF16)
    dims = (message_ref.shape[0], 96)
    at, source = iota(dims, 0), iota(dims, 1)
    spread = jnp.where((at >> 3 == source & 31) & (at & 7 == source >> 5), 1.0, 0.0).astype(BF16)
    message_ref[:, GW:] = dot(spread, jnp.concatenate([high, low, lowest], axis=0)).astype(BF16)
    sums_at = (slice(None), pl.ds(GW, TOK))
    last = pltpu.make_async_copy(
        message_ref.at[sums_at], message_hbm.at[sums_at], message_sem.at[1, 0]
    )
    last.start()
    put_y.wait_all()
    put.wait_all()
    put_message.wait_all()
    last.wait()


def attention_kernel(
    lengths_ref,
    moved_ref,
    values_hbm,
    probs_hbm,
    home_hbm,
    attn_hbm,
    packed_hbm,
    dscores_hbm,
    values_ref,
    probs_ref,
    home_ref,
    attn_ref,
    packed_ref,
    dscores_ref,
    sem,
    out_sem,
):
    fetch = Copies(
        sem,
        (probs_hbm, probs_ref, by_head),
        (values_hbm, values_ref, by_lane),
        (home_hbm, home_ref, by_lane),
    )
    put = Copies(
        out_sem,
        (packed_ref, packed_hbm, by_lane),
        (attn_ref, attn_hbm, by_lane, by_lane_top),
        (dscores_ref, dscores_hbm, by_head),
    )
    scale = 1.0 / math.sqrt(ASIZE)
    fetch.start_all()
    docs = documents(lengths_ref, moved_ref)
    pick = place_slots(docs, (SEND, TOK), 1) == iota((SEND, TOK), 0)
    pick = jnp.where(pick, 1.0, 0.0).astype(BF16)
    kept = jnp.where(place_slots(docs, (TOK, TOK), 0) < 0, 1.0, 0.0).astype(BF16)[:, :1]
    masks = lane_masks()

    def group(g, carry):
        at = lanes(g)
        fetch.wait(g)
        values, grad = values_ref[:, at], home_ref[:, at]
        outs = []
        for i, (tile, count) in enumerate(WINDOWS):
            window = slice(128 * tile, 128 * (tile + count))
            probs = probs_ref[AH * g + i]
            vals = values[:, window] * masks[i]
            outs.append(dot(probs.astype(BF16), vals))
            dprobs = dot(grad[:, window], vals, NT)
            delta = jnp.sum(probs * dprobs, axis=-1, keepdims=True)
            dscores_ref[AH * g + i] = (probs * (dprobs - delta) * scale).astype(BF16)
        head_out = join_windows(outs).astype(BF16)
        attn_ref[:, at] = head_out * kept
        packed_ref[:, at] = dot(pick, head_out).astype(BF16)
        put.start(g)
        return carry

    each_group(group, 0)
    put.wait_all()


def attention_grad_kernel(
    after_ref,
    q_hbm,
    k_hbm,
    dscores_hbm,
    arrived_ref,
    attn_in_hbm,
    gq_hbm,
    gk_hbm,
    attn_hbm,
    q_ref,
    k_ref,
    dscores_ref,
    gq_ref,
    gk_ref,
    sem,
    out_sem,
    arrived_sem,
):
    del attn_in_hbm
    del after_ref
    fetch = Copies(
        sem,
        (dscores_hbm, dscores_ref, by_head),
        (k_hbm, k_ref, by_lane),
        (q_hbm, q_ref, by_lane),
        span=2,
    )
    put = Copies(out_sem, (gq_ref, gq_hbm, by_lane), (gk_ref, gk_hbm, by_lane))
    fetch.start_all()
    leave = pltpu.make_async_copy(arrived_ref, attn_hbm.at[pl.ds(TOK, SEND), :], arrived_sem)
    leave.start()
    masks = lane_masks()

    def group(g, carry):
        at = lanes(g)
        fetch.wait(g)
        q, k = q_ref[:, at], k_ref[:, at]
        gqs, gks = [], []
        for i, (tile, count) in enumerate(WINDOWS):
            window = slice(128 * tile, 128 * (tile + count))
            dscores = dscores_ref[AH * g + i]
            gqs.append(dot(dscores, k[:, window] * masks[i]))
            gks.append(dot(dscores, q[:, window] * masks[i], TN))
        gq_ref[:, at] = join_windows(gqs).astype(BF16)
        gk_ref[:, at] = join_windows(gks).astype(BF16)
        put.start(g)
        return carry

    each_group(group, 0)
    leave.wait()
    put.wait_all()


def inner_back_kernel(
    after_ref,
    x_hbm,
    decays_ref,
    in_ref,
    map_ref,
    skips_ref,
    grown_ref,
    start_hbm,
    y_hbm,
    low_hbm,
    dx_hbm,
    flow_ref,
    direct_ref,
    gout_ref,
    gin_ref,
    skip_sum_ref,
    x_ref,
    start_ref,
    y_ref,
    low_ref,
    dx_ref,
    column_ref,
    row_ref,
    sem,
    out_sem,
):
    del after_ref
    fetch = Copies(
        sem,
        (low_hbm, low_ref, by_lane),
        (x_hbm, x_ref, by_lane),
        (start_hbm, start_ref, by_row),
        (y_hbm, y_ref, by_lane),
        span=2,
    )
    put = Copies(out_sem, (dx_ref, dx_hbm, by_lane), span=2)
    fetch.start_all()
    square = (TOK, TOK)
    causal = iota(square, 0) >= iota(square, 1)
    step, running = decays_ref[1], decays_ref[3]
    skips, grown = skips_ref[...], grown_ref[...]
    row_ref[...] = running - jnp.log(step)
    for g, column in enumerate(columns_of(running)):
        column_ref[g] = column
    in_map, map_in = in_ref[...], map_ref[...]
    gram = jnp.where(causal, dot(map_in, in_map, TN), 0.0)
    flow_ref[...] = jnp.zeros_like(flow_ref)
    direct_ref[...] = jnp.zeros_like(direct_ref)
    gout_ref[...] = jnp.zeros_like(gout_ref)

    def group(g, carry):
        gram_grad, skip_sum = carry
        at = lanes(g)
        fetch.wait(g)
        x, low_grad = x_ref[:, at], low_ref[:, at]
        mixed_grad = low_grad.astype(F32)
        wide = expander(g)
        grown_grad = (dot(grown, wide) * mixed_grad).astype(BF16)
        gout_ref[...] += dot(start_ref[rows64(g), :], grown_grad, NT)
        heads = row_ref[chunk(g, 16), :]
        column = column_ref[g]
        inner = []
        for i in range(GH // 2):
            tile = slice(128 * i, 128 * (i + 1))
            both = dot(low_grad[:, tile], pair_rows(x[:, tile]), NT)
            pair = []
            for j in (0, 1):
                decay = local_decay(column, heads, 2 * i + j)
                gram_grad = gram_grad + both[:, TOK * j : TOK * (j + 1)] * decay
                pair.append((decay * gram).astype(BF16))
            inner.append(dot(jnp.concatenate(pair, axis=0), pair_rows(low_grad[:, tile]), TN))
        inner = jnp.concatenate(inner, axis=1)
        wide_skip = dot(skips, wide)[:1]
        x = x.astype(F32)
        dx_ref[:, at] = inner + wide_skip * mixed_grad
        put.start(g)
        product = x * inner
        high, low = split(mixed_grad * (y_ref[:, at] - wide_skip * x) - product)
        flow_ref[...] += dot(high, wide, NT) + dot(low, wide, NT)
        high, low = split(product)
        direct_ref[...] += dot(high, wide, NT) + dot(low, wide, NT)
        high, low = split(jnp.broadcast_to(jnp.sum(mixed_grad * x, axis=0, keepdims=True), (16, GW)))
        skip_sum = skip_sum + dot(high, wide, NT) + dot(low, wide, NT)
        return gram_grad, skip_sum

    gram_grad, skip_sum = each_group(group, (jnp.zeros(square, F32), jnp.zeros((16, TOK), F32)))
    skip_sum_ref[...] = skip_sum[:1]
    gram_grad = jnp.where(causal, gram_grad, 0.0).astype(BF16)
    gout_ref[...] += dot(in_map, gram_grad, NT)
    gin_ref[...] = dot(map_in, gram_grad)
    put.wait_all()


def late_kernel(
    x_ref,
    decays_ref,
    tail_ref,
    in_ref,
    start_ref,
    grad_ref,
    flow_ref,
    direct_ref,
    skip_ref,
    gain_sum_ref,
    step_ref,
    sums_ref,
):
    z, step, neg, running = (decays_ref[i] for i in range(4))
    last = running[:, TOK - 1 :]
    tail = tail_ref[...]
    in_rows = jnp.transpose(in_ref[...].astype(F32)).astype(BF16)
    tail_sum = jnp.zeros((TOK, TOK), F32)
    overlap = jnp.zeros((16, TOK), F32)
    lates = []
    for g in range(GROUPS):
        grad = grad_ref[g * SIZE : (g + 1) * SIZE, :]
        lates.append(dot(in_rows, grad) * dot(tail, expander(g)))
    for g in range(GROUPS):
        at = slice(g * GW, (g + 1) * GW)
        rows = slice(g * SIZE, (g + 1) * SIZE)
        grad = grad_ref[rows, :]
        wide = expander(g)
        high, low = split(x_ref[:, at].astype(F32) * lates[g])
        tail_sum = tail_sum + dot(high, wide, NT) + dot(low, wide, NT)
        both = jnp.sum(start_ref[rows, :].astype(F32) * grad.astype(F32), axis=0, keepdims=True)
        high, low = split(jnp.broadcast_to(both, (16, GW)))
        overlap = overlap + dot(high, wide, NT) + dot(low, wide, NT)
    tail_sum = jnp.transpose(tail_sum)[:SIZE]
    flow = jnp.transpose(flow_ref[...])[:SIZE]
    direct = jnp.transpose(direct_ref[...])[:SIZE]
    overlap = jnp.transpose(jnp.broadcast_to(overlap[:1], (TOK, TOK)))[:SIZE]
    ahead = sums_by(flow - tail_sum, iota((TOK, TOK), 0) >= iota((TOK, TOK), 1))
    ahead = ahead + jnp.sum(tail_sum, axis=1, keepdims=True) + jnp.exp(last) * overlap
    step_grad = (direct + tail_sum) / step + neg * ahead
    raw_grad = step_grad * (1.0 / (1.0 + jnp.exp(-z)))
    step_ref[...] = unpad_heads(raw_grad)
    rate_grad = jnp.sum(neg * step * ahead, axis=1, keepdims=True)
    bias_grad = jnp.sum(raw_grad, axis=1, keepdims=True)
    both = jnp.concatenate([rate_grad, bias_grad], axis=0)
    devices = sums_ref.shape[0]
    skip_sum = skip_ref[...]
    sums_ref[:, 0, 0:TOK] = jnp.transpose(jnp.broadcast_to(both, (TOK, TOK)))[:devices]
    sums_ref[:, 0, TOK : 2 * TOK] = jnp.broadcast_to(skip_sum, (devices, TOK))
    sums_ref[:, 0, 2 * TOK :] = jnp.broadcast_to(gain_sum_ref[...], (devices, TOK))


def late_rows_kernel(
    x_hbm,
    tail_ref,
    in_ref,
    grad_ref,
    dx_hbm,
    gout_ref,
    gin_ref,
    gx_hbm,
    gin_out_ref,
    gout_out_ref,
    x_ref,
    dx_ref,
    gx_ref,
    sem,
    out_sem,
):
    fetch = Copies(sem, (x_hbm, x_ref, by_lane), (dx_hbm, dx_ref, by_lane))
    put = Copies(out_sem, (gx_ref, gx_hbm, by_lane))
    fetch.start_all()
    tail = tail_ref[...]
    in_rows = jnp.transpose(in_ref[...].astype(F32)).astype(BF16)
    gin = gin_ref[...]
    for g in range(GROUPS):
        at = slice(g * GW, (g + 1) * GW)
        grad = grad_ref[g * SIZE : (g + 1) * SIZE, :]
        weight = dot(tail, expander(g))
        late = dot(in_rows, grad) * weight
        fetch.wait(g)
        gin = gin + dot(grad, (x_ref[:, at].astype(F32) * weight).astype(BF16), NT)
        gx_ref[:, at] = (dx_ref[:, at] + late).astype(BF16)
        put.start(g)
    gin_out_ref[...] = gin.astype(BF16)
    gout_out_ref[...] = gout_ref[...].astype(BF16)
    put.wait_all()


def last_kernel(blocks, sums_ref, heads_ref, gain_ref):
    total = jnp.sum(sums_ref[:, 0, : 2 * TOK], axis=0, keepdims=True)
    for row, at in enumerate((0, SIZE, TOK)):
        for g in range(GROUPS):
            piece = total[:, at + 16 * g : at + 16 * g + GH]
            heads_ref[row : row + 1, GH * g : GH * (g + 1)] = piece
    gains = sums_ref[:, 0, 2 * TOK :]
    parts = gains.shape[0] // blocks
    gains = sum(gains[blocks * d : blocks * (d + 1)] for d in range(parts))
    for i in range(WIDTH // TOK):
        gain_ref[pl.ds(TOK * i, TOK)] = gains[i]


MIB = 1024 * 1024
SMEM = pl.BlockSpec(memory_space=pltpu.SMEM)
VMEM = pl.BlockSpec(memory_space=pltpu.VMEM)


def call(kernel, args, outs, scratch=(), mib=32, us=5, aliases=None):
    specs = {
        "v": VMEM,
        "h": pl.BlockSpec(memory_space=pltpu.HBM),
        "a": VMEM,
        "s": SMEM,
    }
    kept = {"v": pltpu.VMEM, "h": pltpu.HBM}
    made = {"v": pltpu.VMEM, "h": pltpu.HBM, "a": jax.ShapeDtypeStruct}
    arrays = [
        pltpu.with_memory_space_constraint(array, kept[space]) if space in kept else array
        for space, array in args
    ]
    return pl.pallas_call(
        kernel,
        name=getattr(kernel, "func", kernel).__name__,
        out_shape=tuple(made[space](dims, dtype) for space, dims, dtype in outs),
        in_specs=[specs[space] for space, _ in args],
        out_specs=tuple(specs[space] for space, _, _ in outs),
        scratch_shapes=list(scratch),
        input_output_aliases=aliases or {},
        compiler_params=pltpu.CompilerParams(vmem_limit_bytes=mib * MIB),
        cost_estimate=pl.CostEstimate(flops=int(us * 1e9), bytes_accessed=8 * MIB, transcendentals=0),
    )(*arrays)


def local(
    mamba_in,
    step_raw,
    state_in,
    state_out,
    log_rate,
    step_bias,
    skip_gain,
    norm_gain,
    doc_lengths,
    doc_moved,
    queries,
    attn_keys,
    attn_grad,
):
    x, raw, q, k, grad = mamba_in[0], step_raw[0], queries[0], attn_keys[0], attn_grad[0]
    in_map, map_in = jnp.transpose(state_in[0]), jnp.transpose(state_out[0])
    tables = [("s", jnp.transpose(doc_lengths[0])), ("s", jnp.transpose(doc_moved[0]))]
    rate, bias, skip = log_rate[None], step_bias[None], skip_gain[None]
    blocks = lax.axis_size("ctx")
    devices = blocks * lax.axis_size("dp")
    rows = 8 * blocks
    swap = [(i, i ^ (blocks // 2)) for i in range(blocks)]
    wide, square, sent = (TOK, WIDTH), (TOK, TOK), (SEND, WIDTH)
    maps, probs_shape = (SIZE, TOK), (GROUPS * AH, TOK, TOK)
    message_shape, states_shape = (rows, GW + 128), (rows, GW)
    decay_scratch = [pltpu.VMEM((GROUPS, TOK, TOK), F32), pltpu.VMEM(maps, F32)]

    def vmem(dims, dtype=BF16):
        return pltpu.VMEM(dims, dtype)

    def sems(*dims):
        return pltpu.SemaphoreType.DMA(dims)

    def exchange(value):
        value = value.reshape(blocks, 8, value.shape[1])
        value = lax.all_to_all(value, "ctx", 0, 0, tiled=True)
        return value.reshape(rows, value.shape[2])

    decays_shape = (4, SIZE, TOK)
    message, decays, tail = call(
        states_kernel,
        [("h", x), ("h", raw), ("h", in_map), ("h", rate), ("h", bias)],
        [("h", message_shape, BF16), ("a", decays_shape, F32), ("a", square, BF16)],
        [
            vmem(wide),
            vmem((HEADS, TOK), F32),
            vmem(maps),
            vmem((1, HEADS), F32),
            vmem((1, HEADS), F32),
            vmem(message_shape),
            sems(1, GROUPS),
            sems(4),
            sems(1, GROUPS),
        ],
        us=3,
    )
    gathered = exchange(message)
    probs, moving = call(
        weights_kernel,
        tables + [("h", q), ("h", k), ("h", grad)],
        [("h", probs_shape, F32), ("h", sent, BF16)],
        [
            vmem(wide),
            vmem(wide),
            vmem(sent),
            vmem(probs_shape, F32),
            sems(2, GROUPS),
            sems(1, GROUPS),
            sems(2),
        ],
        us=5,
    )
    back = lax.ppermute(moving, "ctx", swap)
    firsts, totals = call(
        functools.partial(scan_kernel, blocks, False),
        [("a", gathered)],
        [("a", states_shape, BF16), ("a", (rows, TOK), BF16)],
        [vmem(states_shape, F32)],
        mib=8,
        us=2,
    )
    start = exchange(firsts)
    decays, tail = ("a", decays), ("a", tail)
    inner, grown, skips = call(
        inner_kernel,
        [("h", x), decays, ("a", in_map), ("a", map_in), ("a", skip)],
        [("a", wide, F32), ("a", square, BF16), ("a", (16, TOK), BF16)],
        [vmem(wide)] + decay_scratch + [sems(1, GROUPS)],
        us=5,
    )
    gv, home = call(
        value_grad_kernel,
        tables + [("h", probs), ("h", grad), ("a", back)],
        [("h", wide, BF16), ("h", wide, BF16)],
        [
            vmem(probs_shape, F32),
            vmem(wide),
            vmem(wide),
            vmem(wide),
            sems(2, GROUPS),
            sems(2, GROUPS),
        ],
        us=4,
    )
    y, values, low, message = call(
        norm_kernel,
        [
            ("a", grown),
            ("a", map_in),
            ("a", norm_gain[None]),
            ("a", start),
            ("a", inner),
            ("h", gv),
        ],
        [("h", wide, F32), ("h", wide, BF16), ("h", wide, BF16), ("h", message_shape, BF16)],
        [
            vmem(wide),
            vmem(wide, F32),
            vmem(wide),
            vmem(wide),
            vmem(message_shape),
            vmem(wide, F32),
            vmem((32, TOK), F32),
            sems(1, GROUPS),
            sems(1, GROUPS),
            sems(2, GROUPS),
            sems(2, GROUPS),
        ],
        us=4,
    )
    attn, packed, dscores = call(
        attention_kernel,
        tables + [("h", values), ("h", probs), ("h", home)],
        [("h", (TOK + SEND, WIDTH), BF16), ("h", sent, BF16), ("h", probs_shape, BF16)],
        [
            vmem(wide),
            vmem(probs_shape, F32),
            vmem(wide),
            vmem(wide),
            vmem(sent),
            vmem(probs_shape),
            sems(3, GROUPS),
            sems(3, GROUPS),
        ],
        us=5,
    )
    arrived = lax.ppermute(packed, "ctx", swap)
    received = exchange(message)
    lasts, gain_sum = call(
        functools.partial(scan_kernel, blocks, True),
        [("a", received), ("a", totals)],
        [("a", states_shape, BF16), ("a", (1, TOK), F32)],
        [vmem(states_shape, F32)],
        mib=8,
        us=2,
    )
    state_grad = exchange(lasts)
    dx, *partial = call(
        inner_back_kernel,
        [("a", gain_sum), ("h", x), decays, ("a", in_map), ("a", map_in), ("a", skips), ("a", grown)]
        + [("h", start), ("h", y), ("h", low)],
        [
            ("h", wide, F32),
            ("a", square, F32),
            ("a", square, F32),
            ("a", maps, F32),
            ("a", maps, F32),
            ("a", (1, TOK), F32),
            ("a", wide, BF16),
            ("a", states_shape, BF16),
        ],
        [vmem(wide, F32), vmem(wide), vmem(wide, F32)]
        + decay_scratch
        + [sems(4, GROUPS), sems(1, GROUPS)],
        us=8,
    )
    flow, direct, gout, gin, skip_sum, same_x, same_start = partial
    gstep, sums = call(
        late_kernel,
        [("a", same_x), decays, tail, ("a", in_map), ("a", same_start), ("a", state_grad)]
        + [("a", flow), ("a", direct), ("a", skip_sum), ("a", gain_sum)],
        [("a", (HEADS, TOK), F32), ("a", (devices, 1, 3 * TOK), F32)],
        us=4,
    )
    sums = lax.all_to_all(sums, ("dp", "ctx"), 0, 0, tiled=True)
    gx, gin, gout = call(
        late_rows_kernel,
        [("h", x), tail, ("a", in_map), ("a", state_grad), ("h", dx), ("a", gout), ("a", gin)],
        [("h", wide, BF16), ("a", maps, BF16), ("a", maps, BF16)],
        [vmem(wide), vmem(wide, F32), vmem(wide), sems(2, GROUPS), sems(1, GROUPS)],
        us=3,
    )
    gq, gk, attn = call(
        attention_grad_kernel,
        [("a", gstep), ("h", q), ("h", k), ("h", dscores), ("a", arrived), ("h", attn)],
        [("h", wide, BF16), ("h", wide, BF16), ("h", (TOK + SEND, WIDTH), BF16)],
        [
            vmem(wide),
            vmem(wide),
            vmem(probs_shape),
            vmem(wide),
            vmem(wide),
            sems(3, GROUPS),
            sems(2, GROUPS),
            pltpu.SemaphoreType.DMA,
        ],
        us=6,
        aliases={5: 2},
    )
    heads, gain = call(
        functools.partial(last_kernel, blocks),
        [("a", sums)],
        [("a", (3, HEADS), F32), ("a", (WIDTH,), F32)],
        mib=4,
        us=1,
    )
    return (
        attn[None],
        gq[None],
        gk[None],
        gx[None],
        jnp.transpose(gin)[None],
        jnp.transpose(gout)[None],
        gstep[None],
        heads,
        gain,
    )


def solution(mesh):
    in_specs = (
        P("dp", "ctx", None),
        P("dp", None, "ctx"),
        P("dp", "ctx", None),
        P("dp", "ctx", None),
        P(),
        P(),
        P(),
        P(),
        P("dp", None, None),
        P("dp", None, None),
        P("dp", "ctx", None),
        P("dp", "ctx", None),
        P("dp", "ctx", None),
    )
    out_specs = (
        P("dp", "ctx", None),
        P("dp", "ctx", None),
        P("dp", "ctx", None),
        P("dp", "ctx", None),
        P("dp", "ctx", None),
        P("dp", "ctx", None),
        P("dp", None, "ctx"),
        P(),
        P(),
    )
    return jax.shard_map(local, mesh=mesh, in_specs=in_specs, out_specs=out_specs, check_vma=False)
```
